32 devices in a mesh: prompt: 8 (over y, x, core), sample: 4 (over z).
Axes of the slice: x: 2, y: 2, z: 4, core: 2. Of those that a mesh axis runs over, the one named last changes fastest.
Arguments:
- queries: bfloat16 [8, 4, 4, 8192], P('prompt', 'sample'), may hold values from -24 to 24
- new_kv: bfloat16 [8, 4, 4, 2, 1024], P('prompt', 'sample'), may hold values from -24 to 24
- suffix_kv: bfloat16 [8, 4, 256, 2, 1024], P('prompt', 'sample'), may hold values from -24 to 24
- suffix_len: int32 [8, 4], P('prompt', 'sample'), may hold values from 1 to 256, as said below
- prefix_head: bfloat16 [8, 512, 2, 1024], P('prompt', 'sample'), may hold values from -24 to 24
- prefix_tail: bfloat16 [8, 512, 2, 1024], P('prompt', 'sample'), may hold values from -24 to 24
- prefix_len: int32 [8], replicated, may hold values from 256 to 1024, as said below
Outputs:
- attended: bfloat16 [8, 4, 4, 8192], P('prompt', 'sample')
The draws below stay inside these ranges and needn't reach their ends.
Inputs may be any that keep to these rules, and one draw needn't show every extreme that they name: `suffix_len`: some sample has all 256 slots live and some only one. `prefix_len`: some prompt has all 1024 positions live and some only 256.
All inputs are finite; a program needn't handle non-finite values.
Results may differ from the reference program's by a relative error of at most 0.001.
Values may be sent and summed in bfloat16 or wider, within the bound.
A program may use at most 64 MiB of HBM per device.

```python
import jax
import jax.numpy as jnp
from jax import lax

QH = 64
KVH = 8
HEAD_SIZE = 128
SUF = 256
STEPS = 4
PROMPTS = 8
SAMPLES = 4
HALF = 512
PREFIX = 1024


def kv_pairs(key, dims_shape):
    sample_base = jnp.clip(jax.random.normal(key, dims_shape, jnp.float32), -6.0, 6.0)
    scales = jnp.array([1.0, 4.0], jnp.float32).reshape(2, 1)
    return sample_base * scales


def draw_queries(key, part):
    own_key = jax.random.fold_in(key, 12)
    dims_shape = (PROMPTS, SAMPLES, STEPS, QH, HEAD_SIZE)
    sample_base = 2.0 * jnp.clip(jax.random.normal(own_key, dims_shape, jnp.float32), -6.0, 6.0)
    return sample_base.reshape(PROMPTS, SAMPLES, STEPS, QH * HEAD_SIZE).astype(jnp.bfloat16)


def draw_new_kv(key, part):
    return kv_pairs(jax.random.fold_in(key, 13), (PROMPTS, SAMPLES, STEPS, 2, KVH * HEAD_SIZE)).astype(jnp.bfloat16)


def draw_suffix_kv(key, part):
    return kv_pairs(jax.random.fold_in(key, 14), (PROMPTS, SAMPLES, SUF, 2, KVH * HEAD_SIZE)).astype(jnp.bfloat16)


def draw_prefix_head(key, part):
    sample_base = kv_pairs(jax.random.fold_in(key, 15), (PROMPTS, HALF, 2, KVH * HEAD_SIZE))
    return sample_base.astype(jnp.bfloat16)


def draw_prefix_tail(key, part):
    return kv_pairs(jax.random.fold_in(key, 16), (PROMPTS, HALF, 2, KVH * HEAD_SIZE)).astype(jnp.bfloat16)


def draw_suffix_len(key, part):
    own_key = jax.random.fold_in(key, 17)
    lengths = jax.random.randint(own_key, (PROMPTS * SAMPLES,), 1, SUF + 1)
    first = jax.random.randint(jax.random.fold_in(own_key, 1), (), 0, PROMPTS * SAMPLES)
    second = (first + 1 + jax.random.randint(jax.random.fold_in(own_key, 2), (), 0, PROMPTS * SAMPLES - 1)) % (PROMPTS * SAMPLES)
    lengths = lengths.at[first].set(SUF)
    lengths = lengths.at[second].set(1)
    return lengths.reshape(PROMPTS, SAMPLES).astype(jnp.int32)


def draw_prefix_len(key, part):
    own_key = jax.random.fold_in(key, 18)
    lengths = jax.random.randint(own_key, (PROMPTS,), PREFIX // 4, PREFIX + 1)
    first = jax.random.randint(jax.random.fold_in(own_key, 1), (), 0, PROMPTS)
    second = (first + 1) % PROMPTS
    lengths = lengths.at[first].set(PREFIX)
    lengths = lengths.at[second].set(PREFIX // 4)
    return lengths.astype(jnp.int32)


def setup_inputs(seed: int = 0) -> dict:
    arg_keys = jax.random.split(jax.random.key(seed), 8)
    return {
        "queries": draw_queries(jax.random.fold_in(arg_keys[7], 71), 0),
        "new_kv": draw_new_kv(jax.random.fold_in(arg_keys[7], 71), 0),
        "suffix_kv": draw_suffix_kv(jax.random.fold_in(arg_keys[7], 71), 0),
        "suffix_len": draw_suffix_len(jax.random.fold_in(arg_keys[7], 71), 0),
        "prefix_head": draw_prefix_head(jax.random.fold_in(arg_keys[7], 71), 0),
        "prefix_tail": draw_prefix_tail(jax.random.fold_in(arg_keys[7], 71), 0),
        "prefix_len": draw_prefix_len(jax.random.fold_in(arg_keys[7], 71), 0),
    }


NEG = -1e30


def apply_weights(logit_scores, valid_mask, value_matrix, form):
    masked = jnp.where(valid_mask, logit_scores, NEG)
    maxima = jnp.max(masked, axis=-1)
    weights = jnp.where(valid_mask, jnp.exp(masked - maxima[..., None]), 0.0)
    totals = jnp.sum(weights, axis=-1)
    numerator = jnp.einsum(form, weights, value_matrix, precision=lax.Precision.HIGHEST)
    leading = numerator.shape[:2]
    return (numerator.reshape(leading + (QH, HEAD_SIZE)), maxima.reshape(leading + (QH,)), totals.reshape(leading + (QH,)))


def prefix_terms(query_rows, pairs, start, length):
    sample_count, step_count = query_rows.shape[0], query_rows.shape[1]
    block_len = pairs.shape[0]
    grouped_queries = query_rows.reshape(sample_count, step_count, KVH, QH // KVH, HEAD_SIZE).astype(jnp.float32)
    key_matrix = pairs[:, 0].reshape(block_len, KVH, HEAD_SIZE).astype(jnp.float32)
    value_matrix = pairs[:, 1].reshape(block_len, KVH, HEAD_SIZE).astype(jnp.float32)
    logit_scores = jnp.einsum("rhlxf,vlf->rhlxv", grouped_queries, key_matrix, precision=lax.Precision.HIGHEST) * (HEAD_SIZE ** -0.5)
    valid_mask = (start + jnp.arange(block_len, dtype=jnp.int32)) < length
    return apply_weights(logit_scores, valid_mask, value_matrix, "urpyj,jpi->urpyi")


def suffix_terms(query_rows, cache, fresh, length):
    sample_count, step_count = query_rows.shape[0], query_rows.shape[1]
    slots = cache.shape[1]
    joined = jnp.concatenate([cache, fresh], axis=1)
    total_len = joined.shape[1]
    grouped_queries = query_rows.reshape(sample_count, step_count, KVH, QH // KVH, HEAD_SIZE).astype(jnp.float32)
    key_matrix = joined[:, :, 0].reshape(sample_count, total_len, KVH, HEAD_SIZE).astype(jnp.float32)
    value_matrix = joined[:, :, 1].reshape(sample_count, total_len, KVH, HEAD_SIZE).astype(jnp.float32)
    logit_scores = jnp.einsum("stkgd,slkd->stkgl", grouped_queries, key_matrix, precision=lax.Precision.HIGHEST) * (HEAD_SIZE ** -0.5)
    cache_live = jnp.arange(slots, dtype=jnp.int32)[None, :] < length[:, None]
    steps_live = jnp.arange(step_count, dtype=jnp.int32)[None, :] <= jnp.arange(step_count, dtype=jnp.int32)[:, None]
    valid_mask = jnp.concatenate([
        jnp.broadcast_to(cache_live[:, None, :], (sample_count, step_count, slots)),
        jnp.broadcast_to(steps_live[None], (sample_count, step_count, step_count))], axis=2)
    return apply_weights(logit_scores, valid_mask[:, :, None, None, :], value_matrix, "stkgl,slkd->stkgd")


def join(former, latter):
    maxima = jnp.maximum(former[1], latter[1])
    scale_a = jnp.exp(former[1] - maxima)
    scale_b = jnp.exp(latter[1] - maxima)
    return (former[0] * scale_a[..., None] + latter[0] * scale_b[..., None], maxima, former[2] * scale_a + latter[2] * scale_b)


def reference(queries, new_kv, suffix_kv, suffix_len, prefix_head, prefix_tail, prefix_len):
    def one_prompt(prompt_index):
        query_rows = queries[prompt_index]
        whole = jnp.concatenate([prefix_head[prompt_index], prefix_tail[(prompt_index + 1) % PROMPTS]], axis=0)
        far_part = prefix_terms(query_rows, whole, jnp.int32(0), prefix_len[prompt_index])
        near_part = suffix_terms(query_rows, suffix_kv[prompt_index], new_kv[prompt_index], suffix_len[prompt_index])
        result = join(far_part, near_part)
        attended = (result[0] / result[2][..., None]).astype(jnp.bfloat16)
        return attended.reshape(query_rows.shape)

    return lax.map(one_prompt, jnp.arange(PROMPTS, dtype=jnp.int32))
```

```python
import functools

import jax
import jax.numpy as jnp
from jax import lax
from jax.experimental import pallas as pl
from jax.experimental.pallas import tpu as pltpu
from jax.sharding import PartitionSpec as P

KVH = 8
HEAD_SIZE = 128
NEG = -1e30
FLOOR = -1e29
PAIR = 2
MESH = pl.DeviceIdType.MESH
F32 = jnp.float32
BF16 = jnp.bfloat16


def softmax_sums(rows, pairs, bias):
    scores = lax.dot_general(rows, pairs, (((1,), (1,)), ((), ())), preferred_element_type=F32)
    masked = scores * HEAD_SIZE ** (-0.5) + bias
    maxima = jnp.maximum(jnp.max(masked, axis=1, keepdims=True), FLOOR)
    weights = jnp.exp(masked - maxima)
    totals = jnp.sum(weights, axis=1, keepdims=True)
    weights = pltpu.roll(weights, 1, 1)
    high = weights.astype(BF16)
    low = (weights - high.astype(F32)).astype(BF16)
    numerator = jnp.dot(high, pairs, preferred_element_type=F32) + jnp.dot(
        low, pairs, preferred_element_type=F32
    )
    return numerator, maxima, totals


def put_stats(stats, lane, head, maxima, totals):
    return jnp.where(lane == head, maxima, jnp.where(lane == KVH + head, totals, stats))


def kernel(
    samples, prompts,
    plen_ref, slen_ref, q_ref, new_ref, suf_ref, head_ref, tail_ref, o_ref,
    qall, keys, stage, sufs, nsend, nrecv, ssend, srecv, near,
    lsem, qs_sem, qr_sem, ts_sem, tr_sem, ns_sem, nr_sem, ss_sem, sr_sem,
):
    row, me = lax.axis_index("prompt"), lax.axis_index("sample")
    steps = q_ref.shape[0]
    group = q_ref.shape[1] // (KVH * HEAD_SIZE)
    rows = steps * group
    block = head_ref.shape[0]
    slots = suf_ref.shape[0]
    chunks = KVH // PAIR
    above = lax.rem(row + prompts - 1, prompts)
    below = lax.rem(row + 1, prompts)

    def lanes(g):
        return pl.ds(g * HEAD_SIZE, HEAD_SIZE)

    def local(kind, g):
        source = (tail_ref, suf_ref, new_ref, head_ref)[kind]
        target = (
            lambda: stage.at[g],
            lambda: sufs.at[g, pl.ds(0, slots)],
            lambda: sufs.at[g, pl.ds(slots, steps)],
            lambda: keys.at[g, pl.ds(0, block)],
        )[kind]
        return pltpu.make_async_copy(source.at[:, :, lanes(g)], target(), lsem.at[kind, g])

    for g in range(KVH):
        local(0, g).start()

    barrier = pltpu.get_barrier_semaphore()
    for d in range(1, samples):
        pl.semaphore_signal(
            barrier, inc=1, device_id=(row, lax.rem(me + d, samples)), device_id_type=MESH
        )
    pl.semaphore_signal(barrier, inc=1, device_id=(above, me), device_id_type=MESH)
    pl.semaphore_signal(barrier, inc=1, device_id=(below, me), device_id_type=MESH)

    spare = sufs.shape[1] - slots
    for g in range(KVH):
        sufs[g, pl.ds(slots, spare)] = jnp.zeros((spare, 2, HEAD_SIZE), BF16)
    for g in range(KVH):
        for kind in range(1, 4):
            local(kind, g).start()

    wide = q_ref[...].astype(F32)
    for g in range(KVH):
        parts = [
            wide[:, (g * group + x) * HEAD_SIZE : (g * group + x + 1) * HEAD_SIZE]
            for x in range(group)
        ]
        qall[0, g] = jnp.concatenate(parts, axis=0).astype(BF16)

    pl.semaphore_wait(barrier, samples + 1)

    def heads(c):
        return pl.ds(c * PAIR, PAIR)

    def q_copy(d, c):
        return pltpu.make_async_remote_copy(
            src_ref=qall.at[0, heads(c)], dst_ref=qall.at[d, heads(c)],
            send_sem=qs_sem.at[d, c], recv_sem=qr_sem.at[d, c],
            device_id=(row, lax.rem(me + d, samples)), device_id_type=MESH,
        )

    def t_copy(c):
        return pltpu.make_async_remote_copy(
            src_ref=stage.at[heads(c)], dst_ref=keys.at[heads(c), pl.ds(block, block)],
            send_sem=ts_sem.at[c], recv_sem=tr_sem.at[c],
            device_id=(above, me), device_id_type=MESH,
        )

    def n_copy(d, c):
        return pltpu.make_async_remote_copy(
            src_ref=nsend.at[d, heads(c)], dst_ref=nrecv.at[d, heads(c)],
            send_sem=ns_sem.at[d, c], recv_sem=nr_sem.at[d, c],
            device_id=(row, lax.rem(me + samples - d, samples)), device_id_type=MESH,
        )

    def s_copy(d):
        return pltpu.make_async_remote_copy(
            src_ref=ssend.at[d], dst_ref=srecv.at[d],
            send_sem=ss_sem.at[d], recv_sem=sr_sem.at[d],
            device_id=(row, lax.rem(me + samples - d, samples)), device_id_type=MESH,
        )

    for c in range(chunks):
        for d in range(1, samples):
            q_copy(d, c).start()
        for g in range(c * PAIR, (c + 1) * PAIR):
            local(0, g).wait()
        t_copy(c).start()

    shape = (rows, 2 * sufs.shape[1])
    column = lax.broadcasted_iota(jnp.int32, shape, 1)
    step = lax.rem(lax.broadcasted_iota(jnp.int32, shape, 0), steps)
    place = column // 2
    live = (place < slen_ref[0, 0]) | ((place >= slots) & (place - slots <= step))
    near_bias = jnp.where(live & (lax.rem(column, 2) == 0), 0.0, NEG).astype(F32)
    lane = lax.broadcasted_iota(jnp.int32, (rows, HEAD_SIZE), 1)

    def near_head(g, stats):
        for kind in range(1, 3):
            local(kind, g).wait()
        pairs = sufs.at[g].reshape(2 * sufs.shape[1], HEAD_SIZE)[...]
        numerator, maxima, totals = softmax_sums(qall[0, g], pairs, near_bias)
        near[g] = numerator
        return put_stats(stats, lane, g, maxima, totals)

    near_stats = lax.fori_loop(0, KVH, near_head, jnp.full((rows, HEAD_SIZE), 0.0, F32))

    column = lax.broadcasted_iota(jnp.int32, (1, 4 * block), 1)
    place = column // 2
    place = jnp.where(place < block, place + me * block, place + (samples + me - 1) * block)
    far_bias = jnp.where((place < plen_ref[row]) & (lax.rem(column, 2) == 0), 0.0, NEG).astype(F32)
    every = samples * rows
    far_lane = lax.broadcasted_iota(jnp.int32, (every, HEAD_SIZE), 1)

    def far_chunk(c, stats):
        for d in range(1, samples):
            q_copy(d, c).wait_recv()
        t_copy(c).wait_recv()
        for i in range(PAIR):
            g = c * PAIR + i
            local(3, g).wait()
            pairs = keys.at[g].reshape(4 * block, HEAD_SIZE)[...]
            queries = qall[:, g].reshape(every, HEAD_SIZE)
            numerator, maxima, totals = softmax_sums(queries, pairs, far_bias)
            nsend[:, g] = numerator.reshape(samples, rows, HEAD_SIZE)
            stats = put_stats(stats, far_lane, g, maxima, totals)
        for d in range(1, samples):
            n_copy(d, c).start()
        return stats

    far_stats = lax.fori_loop(0, chunks, far_chunk, jnp.full((every, HEAD_SIZE), 0.0, F32))
    ssend[...] = far_stats.reshape(samples, rows, HEAD_SIZE)
    for d in range(1, samples):
        s_copy(d).start()
    for d in range(1, samples):
        s_copy(d).wait_recv()

    stats = [near_stats, ssend[0]] + [srecv[d] for d in range(1, samples)]
    peak = functools.reduce(jnp.maximum, stats)
    factors = [jnp.exp(s - peak) for s in stats]
    total = sum(pltpu.roll(s, HEAD_SIZE - KVH, 1) * f for s, f in zip(stats, factors))
    factors = [f / total for f in factors]

    for c in range(chunks):
        for d in range(1, samples):
            n_copy(d, c).wait_recv()
        for g in range(c * PAIR, (c + 1) * PAIR):
            result = near[g] * factors[0][:, g : g + 1] + nsend[0, g] * factors[1][:, g : g + 1]
            for d in range(1, samples):
                result = result + nrecv[d, g] * factors[d + 1][:, g : g + 1]
            o_ref[g] = result.astype(BF16)

    for c in range(chunks):
        t_copy(c).wait_send()
        for d in range(1, samples):
            q_copy(d, c).wait_send()
            n_copy(d, c).wait_send()
    for d in range(1, samples):
        s_copy(d).wait_send()


def per_device(queries, new_kv, suffix_kv, suffix_len, prefix_head, prefix_tail, prefix_len):
    samples = lax.axis_size("sample")
    prompts = lax.axis_size("prompt")
    steps, width = queries.shape[2:]
    group = width // (KVH * HEAD_SIZE)
    rows = steps * group
    block = prefix_head.shape[1]
    slots = suffix_kv.shape[2]
    chunks = KVH // PAIR
    near_len = slots + HEAD_SIZE // 2
    sem = pltpu.SemaphoreType.DMA
    attended = pl.pallas_call(
        functools.partial(kernel, samples, prompts),
        out_shape=jax.ShapeDtypeStruct((KVH, rows, HEAD_SIZE), BF16),
        in_specs=[pl.BlockSpec(memory_space=pltpu.SMEM)] * 2
        + [pl.BlockSpec(memory_space=pltpu.VMEM)]
        + [pl.BlockSpec(memory_space=pl.ANY)] * 4,
        out_specs=pl.BlockSpec(memory_space=pltpu.VMEM),
        scratch_shapes=[
            pltpu.VMEM((samples, KVH, rows, HEAD_SIZE), BF16),
            pltpu.VMEM((KVH, 2 * block, 2, HEAD_SIZE), BF16),
            pltpu.VMEM((KVH, block, 2, HEAD_SIZE), BF16),
            pltpu.VMEM((KVH, near_len, 2, HEAD_SIZE), BF16),
            pltpu.VMEM((samples, KVH, rows, HEAD_SIZE), F32),
            pltpu.VMEM((samples, KVH, rows, HEAD_SIZE), F32),
            pltpu.VMEM((samples, rows, HEAD_SIZE), F32),
            pltpu.VMEM((samples, rows, HEAD_SIZE), F32),
            pltpu.VMEM((KVH, rows, HEAD_SIZE), F32),
            sem((4, KVH)),
            sem((samples, chunks)), sem((samples, chunks)),
            sem((chunks,)), sem((chunks,)),
            sem((samples, chunks)), sem((samples, chunks)),
            sem((samples,)), sem((samples,)),
        ],
        compiler_params=pltpu.CompilerParams(
            collective_id=0, has_side_effects=True, vmem_limit_bytes=48 * 1024 * 1024
        ),
    )(
        prefix_len, suffix_len, queries[0, 0], new_kv[0, 0], suffix_kv[0, 0],
        prefix_head[0], prefix_tail[0],
    )
    attended = attended.reshape(KVH, group, steps, HEAD_SIZE).transpose(2, 0, 1, 3)
    return attended.reshape(queries.shape)


def solution(mesh):
    in_specs = (
        P("prompt", "sample", None, None),
        P("prompt", "sample", None, None, None),
        P("prompt", "sample", None, None, None),
        P("prompt", "sample"),
        P("prompt", "sample", None, None),
        P("prompt", "sample", None, None),
        P(),
    )
    out_specs = P("prompt", "sample", None, None)
    return jax.shard_map(
        per_device, mesh=mesh, in_specs=in_specs, out_specs=out_specs, check_vma=False
    )
```

```python
import functools

import jax
import jax.numpy as jnp
from jax import lax
from jax.experimental import pallas as pl
from jax.experimental.pallas import tpu as pltpu
from jax.sharding import PartitionSpec as P

KVH = 8
HEAD_SIZE = 128
NEG = -1e30
FLOOR = -1e29
PAIR = 2
MESH = pl.DeviceIdType.MESH
F32 = jnp.float32
BF16 = jnp.bfloat16


def softmax_sums(rows, pairs, bias):
    scores = lax.dot_general(rows, pairs, (((1,), (1,)), ((), ())), preferred_element_type=F32)
    masked = scores * HEAD_SIZE ** (-0.5) + bias
    maxima = jnp.maximum(jnp.max(masked, axis=1, keepdims=True), FLOOR)
    weights = jnp.exp(masked - maxima)
    totals = jnp.sum(weights, axis=1, keepdims=True)
    weights = pltpu.roll(weights, 1, 1)
    high = weights.astype(BF16)
    low = (weights - high.astype(F32)).astype(BF16)
    numerator = jnp.dot(high, pairs, preferred_element_type=F32) + jnp.dot(
        low, pairs, preferred_element_type=F32
    )
    return numerator, maxima, totals


def put_stats(stats, lane, head, maxima, totals):
    return jnp.where(lane == head, maxima, jnp.where(lane == KVH + head, totals, stats))


def kernel(
    samples, prompts,
    plen_hbm, slen_hbm, q_hbm, new_ref, suf_ref, head_ref, tail_ref, o_ref,
    plen_ref, slen_ref, q_ref, qall, keys, stage, sufs, nsend, nrecv, ssend, srecv, near,
    asem, lsem, qs_sem, qr_sem, ts_sem, tr_sem, ns_sem, nr_sem, ss_sem, sr_sem,
):
    row, me = lax.axis_index("prompt"), lax.axis_index("sample")
    steps = q_ref.shape[0]
    group = q_ref.shape[1] // (KVH * HEAD_SIZE)
    rows = steps * group
    block = head_ref.shape[0]
    slots = suf_ref.shape[0]
    chunks = KVH // PAIR
    above = lax.rem(row + prompts - 1, prompts)
    below = lax.rem(row + 1, prompts)

    def lanes(g):
        return pl.ds(g * HEAD_SIZE, HEAD_SIZE)

    def local(kind, g):
        source = (tail_ref, suf_ref, new_ref, head_ref)[kind]
        target = (
            lambda: stage.at[g],
            lambda: sufs.at[g, pl.ds(0, slots)],
            lambda: sufs.at[g, pl.ds(slots, steps)],
            lambda: keys.at[g, pl.ds(0, block)],
        )[kind]
        return pltpu.make_async_copy(source.at[:, :, lanes(g)], target(), lsem.at[kind, g])

    arrivals = [
        pltpu.make_async_copy(q_hbm, q_ref, asem.at[0]),
        pltpu.make_async_copy(plen_hbm, plen_ref, asem.at[1]),
        pltpu.make_async_copy(slen_hbm, slen_ref, asem.at[2]),
    ]
    for copy in arrivals:
        copy.start()
    for g in range(KVH):
        local(0, g).start()

    barrier = pltpu.get_barrier_semaphore()
    for d in range(1, samples):
        pl.semaphore_signal(
            barrier, inc=1, device_id=(row, lax.rem(me + d, samples)), device_id_type=MESH
        )
    pl.semaphore_signal(barrier, inc=1, device_id=(above, me), device_id_type=MESH)
    pl.semaphore_signal(barrier, inc=1, device_id=(below, me), device_id_type=MESH)

    spare = sufs.shape[1] - slots
    for g in range(KVH):
        sufs[g, pl.ds(slots, spare)] = jnp.zeros((spare, 2, HEAD_SIZE), BF16)
    for g in range(KVH):
        for kind in range(1, 4):
            local(kind, g).start()

    for copy in arrivals:
        copy.wait()
    wide = q_ref[...].astype(F32)
    for g in range(KVH):
        parts = [
            wide[:, (g * group + x) * HEAD_SIZE : (g * group + x + 1) * HEAD_SIZE]
            for x in range(group)
        ]
        qall[0, g] = jnp.concatenate(parts, axis=0).astype(BF16)

    pl.semaphore_wait(barrier, samples + 1)

    def heads(c):
        return pl.ds(c * PAIR, PAIR)

    def q_copy(d, c):
        return pltpu.make_async_remote_copy(
            src_ref=qall.at[0, heads(c)], dst_ref=qall.at[d, heads(c)],
            send_sem=qs_sem.at[d, c], recv_sem=qr_sem.at[d, c],
            device_id=(row, lax.rem(me + d, samples)), device_id_type=MESH,
        )

    def t_copy(c):
        return pltpu.make_async_remote_copy(
            src_ref=stage.at[heads(c)], dst_ref=keys.at[heads(c), pl.ds(block, block)],
            send_sem=ts_sem.at[c], recv_sem=tr_sem.at[c],
            device_id=(above, me), device_id_type=MESH,
        )

    def n_copy(d, c):
        return pltpu.make_async_remote_copy(
            src_ref=nsend.at[d, heads(c)], dst_ref=nrecv.at[d, heads(c)],
            send_sem=ns_sem.at[d, c], recv_sem=nr_sem.at[d, c],
            device_id=(row, lax.rem(me + samples - d, samples)), device_id_type=MESH,
        )

    def s_copy(d):
        return pltpu.make_async_remote_copy(
            src_ref=ssend.at[d], dst_ref=srecv.at[d],
            send_sem=ss_sem.at[d], recv_sem=sr_sem.at[d],
            device_id=(row, lax.rem(me + samples - d, samples)), device_id_type=MESH,
        )

    for c in range(chunks):
        for d in range(1, samples):
            q_copy(d, c).start()
        for g in range(c * PAIR, (c + 1) * PAIR):
            local(0, g).wait()
        t_copy(c).start()

    shape = (rows, 2 * sufs.shape[1])
    column = lax.broadcasted_iota(jnp.int32, shape, 1)
    step = lax.rem(lax.broadcasted_iota(jnp.int32, shape, 0), steps)
    place = column // 2
    live = (place < slen_ref[0, 0]) | ((place >= slots) & (place - slots <= step))
    near_bias = jnp.where(live & (lax.rem(column, 2) == 0), 0.0, NEG).astype(F32)
    lane = lax.broadcasted_iota(jnp.int32, (rows, HEAD_SIZE), 1)

    def near_head(g, stats):
        for kind in range(1, 3):
            local(kind, g).wait()
        pairs = sufs.at[g].reshape(2 * sufs.shape[1], HEAD_SIZE)[...]
        numerator, maxima, totals = softmax_sums(qall[0, g], pairs, near_bias)
        near[g] = numerator
        return put_stats(stats, lane, g, maxima, totals)

    near_stats = lax.fori_loop(0, KVH, near_head, jnp.full((rows, HEAD_SIZE), 0.0, F32))

    column = lax.broadcasted_iota(jnp.int32, (1, 4 * block), 1)
    place = column // 2
    place = jnp.where(place < block, place + me * block, place + (samples + me - 1) * block)
    far_bias = jnp.where((place < plen_ref[row]) & (lax.rem(column, 2) == 0), 0.0, NEG).astype(F32)
    every = samples * rows
    far_lane = lax.broadcasted_iota(jnp.int32, (every, HEAD_SIZE), 1)

    def far_chunk(c, stats):
        for d in range(1, samples):
            q_copy(d, c).wait_recv()
        t_copy(c).wait_recv()
        for i in range(PAIR):
            g = c * PAIR + i
            local(3, g).wait()
            pairs = keys.at[g].reshape(4 * block, HEAD_SIZE)[...]
            queries = qall[:, g].reshape(every, HEAD_SIZE)
            numerator, maxima, totals = softmax_sums(queries, pairs, far_bias)
            nsend[:, g] = numerator.reshape(samples, rows, HEAD_SIZE)
            stats = put_stats(stats, far_lane, g, maxima, totals)
        for d in range(1, samples):
            n_copy(d, c).start()
        return stats

    far_stats = lax.fori_loop(0, chunks, far_chunk, jnp.full((every, HEAD_SIZE), 0.0, F32))
    ssend[...] = far_stats.reshape(samples, rows, HEAD_SIZE)
    for d in range(1, samples):
        s_copy(d).start()
    for d in range(1, samples):
        s_copy(d).wait_recv()

    stats = [near_stats, ssend[0]] + [srecv[d] for d in range(1, samples)]
    peak = functools.reduce(jnp.maximum, stats)
    factors = [jnp.exp(s - peak) for s in stats]
    total = sum(pltpu.roll(s, HEAD_SIZE - KVH, 1) * f for s, f in zip(stats, factors))
    factors = [f / total for f in factors]

    for c in range(chunks):
        for d in range(1, samples):
            n_copy(d, c).wait_recv()
        for g in range(c * PAIR, (c + 1) * PAIR):
            result = near[g] * factors[0][:, g : g + 1] + nsend[0, g] * factors[1][:, g : g + 1]
            for d in range(1, samples):
                result = result + nrecv[d, g] * factors[d + 1][:, g : g + 1]
            o_ref[g] = result.astype(BF16)

    for c in range(chunks):
        t_copy(c).wait_send()
        for d in range(1, samples):
            q_copy(d, c).wait_send()
            n_copy(d, c).wait_send()
    for d in range(1, samples):
        s_copy(d).wait_send()


def per_device(queries, new_kv, suffix_kv, suffix_len, prefix_head, prefix_tail, prefix_len):
    samples = lax.axis_size("sample")
    prompts = lax.axis_size("prompt")
    steps, width = queries.shape[2:]
    group = width // (KVH * HEAD_SIZE)
    rows = steps * group
    block = prefix_head.shape[1]
    slots = suffix_kv.shape[2]
    chunks = KVH // PAIR
    near_len = slots + HEAD_SIZE // 2
    sem = pltpu.SemaphoreType.DMA
    attended = pl.pallas_call(
        functools.partial(kernel, samples, prompts),
        out_shape=jax.ShapeDtypeStruct((KVH, rows, HEAD_SIZE), BF16),
        in_specs=[pl.BlockSpec(memory_space=pl.ANY)] * 7,
        out_specs=pl.BlockSpec(memory_space=pltpu.VMEM),
        scratch_shapes=[
            pltpu.SMEM(prefix_len.shape, jnp.int32),
            pltpu.SMEM(suffix_len.shape, jnp.int32),
            pltpu.VMEM((steps, width), BF16),
            pltpu.VMEM((samples, KVH, rows, HEAD_SIZE), BF16),
            pltpu.VMEM((KVH, 2 * block, 2, HEAD_SIZE), BF16),
            pltpu.VMEM((KVH, block, 2, HEAD_SIZE), BF16),
            pltpu.VMEM((KVH, near_len, 2, HEAD_SIZE), BF16),
            pltpu.VMEM((samples, KVH, rows, HEAD_SIZE), F32),
            pltpu.VMEM((samples, KVH, rows, HEAD_SIZE), F32),
            pltpu.VMEM((samples, rows, HEAD_SIZE), F32),
            pltpu.VMEM((samples, rows, HEAD_SIZE), F32),
            pltpu.VMEM((KVH, rows, HEAD_SIZE), F32),
            sem((3,)), sem((4, KVH)),
            sem((samples, chunks)), sem((samples, chunks)),
            sem((chunks,)), sem((chunks,)),
            sem((samples, chunks)), sem((samples, chunks)),
            sem((samples,)), sem((samples,)),
        ],
        compiler_params=pltpu.CompilerParams(
            collective_id=0, has_side_effects=True, vmem_limit_bytes=64 * 1024 * 1024
        ),
    )(
        prefix_len, suffix_len, queries[0, 0], new_kv[0, 0], suffix_kv[0, 0],
        prefix_head[0], prefix_tail[0],
    )
    attended = attended.reshape(KVH, group, steps, HEAD_SIZE).transpose(2, 0, 1, 3)
    return attended.reshape(queries.shape)


def solution(mesh):
    in_specs = (
        P("prompt", "sample", None, None),
        P("prompt", "sample", None, None, None),
        P("prompt", "sample", None, None, None),
        P("prompt", "sample"),
        P("prompt", "sample", None, None),
        P("prompt", "sample", None, None),
        P(),
    )
    out_specs = P("prompt", "sample", None, None)
    return jax.shard_map(
        per_device, mesh=mesh, in_specs=in_specs, out_specs=out_specs, check_vma=False
    )
```

```python
import functools

import jax
import jax.numpy as jnp
from jax import lax
from jax.experimental import pallas as pl
from jax.experimental.pallas import tpu as pltpu
from jax.sharding import PartitionSpec as P

KVH = 8
HEAD_SIZE = 128
NEG = -1e30
FLOOR = -1e29
PAIR = 2
MESH = pl.DeviceIdType.MESH
F32 = jnp.float32
BF16 = jnp.bfloat16


def softmax_sums(rows, pairs, bias):
    scores = lax.dot_general(rows, pairs, (((1,), (1,)), ((), ())), preferred_element_type=F32)
    masked = scores * HEAD_SIZE ** (-0.5) + bias
    maxima = jnp.maximum(jnp.max(masked, axis=1, keepdims=True), FLOOR)
    weights = jnp.exp(masked - maxima)
    totals = jnp.sum(weights, axis=1, keepdims=True)
    weights = pltpu.roll(weights, 1, 1)
    high = weights.astype(BF16)
    low = (weights - high.astype(F32)).astype(BF16)
    numerator = jnp.dot(high, pairs, preferred_element_type=F32) + jnp.dot(
        low, pairs, preferred_element_type=F32
    )
    return numerator, maxima, totals


def as_rows(columns):
    count = columns[0].shape[0]
    lane = lax.broadcasted_iota(jnp.int32, (count, HEAD_SIZE), 1)
    tile = jnp.zeros((count, HEAD_SIZE), F32)
    for i, column in enumerate(columns):
        tile = jnp.where(lane == i, column, tile)
    if count < HEAD_SIZE:
        tile = jnp.concatenate([tile, jnp.zeros((HEAD_SIZE - count, HEAD_SIZE), F32)], axis=0)
    return tile.T[:8]


def join_rows(tiles):
    peak = functools.reduce(jnp.maximum, tiles)
    factors = [jnp.exp(t - peak) for t in tiles]
    totals = sum(t * pltpu.roll(f, PAIR, 0) for t, f in zip(tiles, factors))
    return peak, totals, factors


def as_columns(factors):
    row = lax.broadcasted_iota(jnp.int32, factors[0].shape, 0)
    columns = []
    for start in range(0, len(factors), 8 // PAIR):
        few = factors[start : start + 8 // PAIR]
        packed = few[0]
        for k in range(1, len(few)):
            packed = jnp.where(row < k * PAIR, packed, pltpu.roll(few[k], k * PAIR, 0))
        turned = packed.T
        for k in range(len(few)):
            columns.append([turned[:, k * PAIR + i : k * PAIR + i + 1] for i in range(PAIR)])
    return columns


def kernel(
    samples, prompts,
    plen_hbm, slen_hbm, q_hbm, new_ref, suf_ref, head_ref, tail_ref, o_ref,
    plen_ref, slen_ref, q_ref, qall, keys, stage, sufs,
    near, near_rows, nbuf, sbuf, n1, s1, cbuf, tbuf, n2, s2,
    asem, lsem, qs_sem, qr_sem, ts_sem, tr_sem, p_sem, f_sem,
):
    row, me = lax.axis_index("prompt"), lax.axis_index("sample")
    steps = q_ref.shape[0]
    group = q_ref.shape[1] // (KVH * HEAD_SIZE)
    rows = steps * group
    block = head_ref.shape[0]
    slots = suf_ref.shape[0]
    chunks = KVH // PAIR
    above = lax.rem(row + prompts - 1, prompts)
    below = lax.rem(row + 1, prompts)
    half = samples // 2

    def peer(x):
        other, bit = 0, 1
        while bit < samples:
            digit = lax.rem(me // bit, 2)
            other = other + bit * (1 - digit if x & bit else digit)
            bit *= 2
        return other

    def place_of(x):
        return (x % 2) * half + x // 2

    def lanes(g):
        return pl.ds(g * HEAD_SIZE, HEAD_SIZE)

    def local(kind, g):
        source = (tail_ref, suf_ref, new_ref, head_ref)[kind]
        target = (
            lambda: stage.at[g],
            lambda: sufs.at[g, pl.ds(0, slots)],
            lambda: sufs.at[g, pl.ds(slots, steps)],
            lambda: keys.at[g, pl.ds(0, block)],
        )[kind]
        return pltpu.make_async_copy(source.at[:, :, lanes(g)], target(), lsem.at[kind, g])

    arrivals = [
        pltpu.make_async_copy(q_hbm, q_ref, asem.at[0]),
        pltpu.make_async_copy(plen_hbm, plen_ref, asem.at[1]),
        pltpu.make_async_copy(slen_hbm, slen_ref, asem.at[2]),
    ]
    for copy in arrivals:
        copy.start()
    for g in range(KVH):
        local(0, g).start()

    barrier = pltpu.get_barrier_semaphore()
    for x in range(1, samples):
        pl.semaphore_signal(barrier, inc=1, device_id=(row, peer(x)), device_id_type=MESH)
    pl.semaphore_signal(barrier, inc=1, device_id=(above, me), device_id_type=MESH)
    pl.semaphore_signal(barrier, inc=1, device_id=(below, me), device_id_type=MESH)

    spare = sufs.shape[1] - slots
    for g in range(KVH):
        sufs[g, pl.ds(slots, spare)] = jnp.zeros((spare, 2, HEAD_SIZE), BF16)
    for g in range(KVH):
        for kind in range(1, 4):
            local(kind, g).start()

    for copy in arrivals:
        copy.wait()
    wide = q_ref[...].astype(F32)
    for g in range(KVH):
        parts = [
            wide[:, (g * group + x) * HEAD_SIZE : (g * group + x + 1) * HEAD_SIZE]
            for x in range(group)
        ]
        qall[0, g] = jnp.concatenate(parts, axis=0).astype(BF16)

    pl.semaphore_wait(barrier, samples + 1)

    def heads(c):
        return pl.ds(c * PAIR, PAIR)

    def remote(source, target, send, recv, device):
        return pltpu.make_async_remote_copy(
            src_ref=source, dst_ref=target, send_sem=send, recv_sem=recv,
            device_id=device, device_id_type=MESH,
        )

    def q_copy(x, c):
        i = place_of(x)
        return remote(
            qall.at[0, heads(c)], qall.at[i, heads(c)],
            qs_sem.at[i, c], qr_sem.at[i, c], (row, peer(x)),
        )

    def t_copy(c):
        return remote(
            stage.at[heads(c)], keys.at[heads(c), pl.ds(block, block)],
            ts_sem.at[c], tr_sem.at[c], (above, me),
        )

    def pair_sums(c):
        return remote(
            nbuf.at[c, pl.ds(half, half)], n1.at[c], p_sem.at[0, c], p_sem.at[1, c], (row, peer(1))
        )

    def pair_stats(c):
        return remote(sbuf.at[c], s1.at[c], p_sem.at[2, c], p_sem.at[3, c], (row, peer(1)))

    def far_sums(e, c):
        return remote(
            cbuf.at[c, e], n2.at[c, e], f_sem.at[0, e, c], f_sem.at[1, e, c], (row, peer(2 * e))
        )

    def far_stats(e, c):
        return remote(
            tbuf.at[c], s2.at[c, e], f_sem.at[2, e, c], f_sem.at[3, e, c], (row, peer(2 * e))
        )

    for c in range(chunks):
        for x in range(1, samples):
            q_copy(x, c).start()
        for g in range(c * PAIR, (c + 1) * PAIR):
            local(0, g).wait()
        t_copy(c).start()

    shape = (rows, 2 * sufs.shape[1])
    column = lax.broadcasted_iota(jnp.int32, shape, 1)
    step = lax.rem(lax.broadcasted_iota(jnp.int32, shape, 0), steps)
    place = column // 2
    live = (place < slen_ref[0, 0]) | ((place >= slots) & (place - slots <= step))
    near_bias = jnp.where(live & (lax.rem(column, 2) == 0), 0.0, NEG).astype(F32)

    def near_chunk(c, carry):
        maxima, totals = [], []
        for i in range(PAIR):
            g = c * PAIR + i
            for kind in range(1, 3):
                local(kind, g).wait()
            pairs = sufs.at[g].reshape(2 * sufs.shape[1], HEAD_SIZE)[...]
            near[g], top, total = softmax_sums(qall[0, g], pairs, near_bias)
            maxima.append(top)
            totals.append(total)
        near_rows[c] = as_rows(maxima + totals)
        return carry

    lax.fori_loop(0, chunks, near_chunk, 0)

    column = lax.broadcasted_iota(jnp.int32, (1, 4 * block), 1)
    place = column // 2
    place = jnp.where(place < block, place + me * block, place + (samples + me - 1) * block)
    far_bias = jnp.where((place < plen_ref[row]) & (lax.rem(column, 2) == 0), 0.0, NEG).astype(F32)
    every = samples * rows

    def partial(c):
        for x in range(1, samples):
            q_copy(x, c).wait_recv()
        t_copy(c).wait_recv()
        maxima, totals = [], []
        for i in range(PAIR):
            g = c * PAIR + i
            local(3, g).wait()
            pairs = keys.at[g].reshape(4 * block, HEAD_SIZE)[...]
            queries = qall[:, g].reshape(every, HEAD_SIZE)
            numerator, top, total = softmax_sums(queries, pairs, far_bias)
            nbuf[c, :, i] = numerator.reshape(samples, rows, HEAD_SIZE)
            maxima.append(top)
            totals.append(total)
        pair_sums(c).start()
        sbuf[c] = as_rows(maxima + totals)
        pair_stats(c).start()

    def join_pair(c):
        pair_stats(c).wait_recv()
        tiles = [sbuf[c], pltpu.roll(s1[c], every // 2, 1)]
        peak, totals, factors = join_rows(tiles)
        rank = lax.broadcasted_iota(jnp.int32, peak.shape, 0)
        tbuf[c] = jnp.where(rank < PAIR, peak, totals)
        for e in range(1, half):
            far_stats(e, c).start()
        mine, other = as_columns(factors)
        pair_sums(c).wait_recv()
        for e in list(range(1, half)) + [0]:
            span = slice(e * rows, (e + 1) * rows)
            for i in range(PAIR):
                cbuf[c, e, i] = nbuf[c, e, i] * mine[i][span] + n1[c, e, i] * other[i][span]
            if e:
                far_sums(e, c).start()

    def finish(c):
        tiles = [near_rows[c], tbuf[c][:, :HEAD_SIZE]]
        for e in range(1, half):
            far_stats(e, c).wait_recv()
            tiles.append(pltpu.roll(s2[c, e], every - e * rows, 1)[:, :HEAD_SIZE])
        _, totals, factors = join_rows(tiles)
        totals = pltpu.roll(totals, 8 - PAIR, 0)
        columns = as_columns([f / totals for f in factors])
        for e in range(1, half):
            far_sums(e, c).wait_recv()
        for i in range(PAIR):
            g = c * PAIR + i
            result = near[g] * columns[0][i][:rows] + cbuf[c, 0, i] * columns[1][i][:rows]
            for e in range(1, half):
                result = result + n2[c, e, i] * columns[e + 1][i][:rows]
            flat = [result[x * steps : (x + 1) * steps] for x in range(group)]
            o_ref[:, g * group * HEAD_SIZE : (g + 1) * group * HEAD_SIZE] = jnp.concatenate(
                flat, axis=1
            ).astype(BF16)

    for c in range(chunks + 2):
        if c < chunks:
            partial(c)
        if 1 <= c <= chunks:
            join_pair(c - 1)
        if c >= 2:
            finish(c - 2)

    for c in range(chunks):
        t_copy(c).wait_send()
        pair_sums(c).wait_send()
        pair_stats(c).wait_send()
        for x in range(1, samples):
            q_copy(x, c).wait_send()
        for e in range(1, half):
            far_sums(e, c).wait_send()
            far_stats(e, c).wait_send()


def per_device(queries, new_kv, suffix_kv, suffix_len, prefix_head, prefix_tail, prefix_len):
    samples = lax.axis_size("sample")
    prompts = lax.axis_size("prompt")
    steps, width = queries.shape[2:]
    group = width // (KVH * HEAD_SIZE)
    rows = steps * group
    block = prefix_head.shape[1]
    slots = suffix_kv.shape[2]
    chunks = KVH // PAIR
    half, every = samples // 2, samples * rows
    near_len = slots + HEAD_SIZE // 2
    sem = pltpu.SemaphoreType.DMA
    attended = pl.pallas_call(
        functools.partial(kernel, samples, prompts),
        out_shape=jax.ShapeDtypeStruct((steps, width), BF16),
        in_specs=[pl.BlockSpec(memory_space=pl.ANY)] * 7,
        out_specs=pl.BlockSpec(memory_space=pltpu.VMEM),
        scratch_shapes=[
            pltpu.SMEM(prefix_len.shape, jnp.int32),
            pltpu.SMEM(suffix_len.shape, jnp.int32),
            pltpu.VMEM((steps, width), BF16),
            pltpu.VMEM((samples, KVH, rows, HEAD_SIZE), BF16),
            pltpu.VMEM((KVH, 2 * block, 2, HEAD_SIZE), BF16),
            pltpu.VMEM((KVH, block, 2, HEAD_SIZE), BF16),
            pltpu.VMEM((KVH, near_len, 2, HEAD_SIZE), BF16),
            pltpu.VMEM((KVH, rows, HEAD_SIZE), F32),
            pltpu.VMEM((chunks, 8, HEAD_SIZE), F32),
            pltpu.VMEM((chunks, samples, PAIR, rows, HEAD_SIZE), F32),
            pltpu.VMEM((chunks, 8, every), F32),
            pltpu.VMEM((chunks, half, PAIR, rows, HEAD_SIZE), F32),
            pltpu.VMEM((chunks, 8, every), F32),
            pltpu.VMEM((chunks, half, PAIR, rows, HEAD_SIZE), F32),
            pltpu.VMEM((chunks, 8, every), F32),
            pltpu.VMEM((chunks, half, PAIR, rows, HEAD_SIZE), F32),
            pltpu.VMEM((chunks, half, 8, every), F32),
            sem((3,)), sem((4, KVH)),
            sem((samples, chunks)), sem((samples, chunks)),
            sem((chunks,)), sem((chunks,)),
            sem((4, chunks)), sem((4, half, chunks)),
        ],
        compiler_params=pltpu.CompilerParams(
            collective_id=0, has_side_effects=True, vmem_limit_bytes=64 * 1024 * 1024
        ),
    )(
        prefix_len, suffix_len, queries[0, 0], new_kv[0, 0], suffix_kv[0, 0],
        prefix_head[0], prefix_tail[0],
    )
    return attended.reshape(queries.shape)


def solution(mesh):
    in_specs = (
        P("prompt", "sample", None, None),
        P("prompt", "sample", None, None, None),
        P("prompt", "sample", None, None, None),
        P("prompt", "sample"),
        P("prompt", "sample", None, None),
        P("prompt", "sample", None, None),
        P(),
    )
    out_specs = P("prompt", "sample", None, None)
    return jax.shard_map(
        per_device, mesh=mesh, in_specs=in_specs, out_specs=out_specs, check_vma=False
    )
```

```python
import functools

import jax
import jax.numpy as jnp
from jax import lax
from jax.experimental import pallas as pl
from jax.experimental.pallas import tpu as pltpu
from jax.sharding import PartitionSpec as P

KVH = 8
HEAD_SIZE = 128
NEG = -1e30
FLOOR = -1e29
PAIR = 2
TILE = 16
MESH = pl.DeviceIdType.MESH
F32 = jnp.float32
BF16 = jnp.bfloat16


def softmax_sums(rows, keys, values, bias):
    scores = lax.dot_general(rows, keys, (((1,), (1,)), ((), ())), preferred_element_type=F32)
    masked = scores * HEAD_SIZE ** (-0.5) + bias
    maxima = jnp.maximum(jnp.max(masked, axis=1, keepdims=True), FLOOR)
    weights = jnp.exp(masked - maxima)
    totals = jnp.sum(weights, axis=1, keepdims=True)
    high = weights.astype(BF16)
    low = (weights - high.astype(F32)).astype(BF16)
    numerator = jnp.dot(high, values, preferred_element_type=F32) + jnp.dot(
        low, values, preferred_element_type=F32
    )
    return numerator, maxima, totals


def permutation():
    size = 2 * KVH * TILE
    to = lax.broadcasted_iota(jnp.int32, (size, size), 0)
    source = lax.rem(to, TILE) * (2 * KVH) + lax.rem(to // TILE, KVH) * 2 + to // (TILE * KVH)
    return (lax.broadcasted_iota(jnp.int32, (size, size), 1) == source).astype(BF16)


def take_apart(order, raw, target, first, count):
    size = 2 * KVH * TILE
    flat = raw.reshape(raw.shape[0] * 2, HEAD_SIZE)

    def one(b, carry):
        block = flat[pl.ds(pl.multiple_of(b * size, size), size)]
        sorted_rows = jnp.dot(order, block, preferred_element_type=F32).astype(BF16)
        for kind in range(2):
            for g in range(KVH):
                at = (kind * KVH + g) * TILE
                target[g, kind, pl.ds(pl.multiple_of(b * TILE, TILE), TILE)] = sorted_rows[at : at + TILE]
        return carry

    lax.fori_loop(first, first + count, one, 0)


def as_rows(columns):
    count = columns[0].shape[0]
    lane = lax.broadcasted_iota(jnp.int32, (count, HEAD_SIZE), 1)
    tile = jnp.zeros((count, HEAD_SIZE), F32)
    for i, column in enumerate(columns):
        tile = jnp.where(lane == i, column, tile)
    if count < HEAD_SIZE:
        tile = jnp.concatenate([tile, jnp.zeros((HEAD_SIZE - count, HEAD_SIZE), F32)], axis=0)
    return tile.T[:8]


def join_rows(tiles):
    peak = functools.reduce(jnp.maximum, tiles)
    factors = [jnp.exp(t - peak) for t in tiles]
    totals = sum(t * pltpu.roll(f, PAIR, 0) for t, f in zip(tiles, factors))
    return peak, totals, factors


def as_columns(factors):
    row = lax.broadcasted_iota(jnp.int32, factors[0].shape, 0)
    columns = []
    for start in range(0, len(factors), 8 // PAIR):
        few = factors[start : start + 8 // PAIR]
        packed = few[0]
        for k in range(1, len(few)):
            packed = jnp.where(row < k * PAIR, packed, pltpu.roll(few[k], k * PAIR, 0))
        turned = packed.T
        for k in range(len(few)):
            columns.append([turned[:, k * PAIR + i : k * PAIR + i + 1] for i in range(PAIR)])
    return columns


def kernel(
    samples, prompts,
    plen_hbm, slen_hbm, q_hbm, new_ref, suf_ref, head_ref, tail_ref, o_ref,
    plen_ref, slen_ref, q_ref, tail_raw, suf_raw, head_raw, qall, keys, stage, sufs,
    near, near_rows, nbuf, sbuf, n1, s1, cbuf, tbuf, n2, s2,
    asem, lsem, qs_sem, qr_sem, ts_sem, tr_sem, p_sem, f_sem,
):
    row, me = lax.axis_index("prompt"), lax.axis_index("sample")
    steps = q_ref.shape[0]
    group = q_ref.shape[1] // (KVH * HEAD_SIZE)
    rows = steps * group
    block = head_ref.shape[0] // KVH
    slots = suf_ref.shape[0] // KVH
    chunks = KVH // PAIR
    above = lax.rem(row + prompts - 1, prompts)
    below = lax.rem(row + 1, prompts)
    half = samples // 2

    def peer(x):
        other, bit = 0, 1
        while bit < samples:
            digit = lax.rem(me // bit, 2)
            other = other + bit * (1 - digit if x & bit else digit)
            bit *= 2
        return other

    def place_of(x):
        return (x % 2) * half + x // 2

    locals_ = [
        pltpu.make_async_copy(tail_ref, tail_raw, lsem.at[0]),
        pltpu.make_async_copy(suf_ref, suf_raw.at[pl.ds(0, slots * KVH)], lsem.at[1]),
        pltpu.make_async_copy(new_ref, suf_raw.at[pl.ds(slots * KVH, steps * KVH)], lsem.at[2]),
        pltpu.make_async_copy(head_ref, head_raw, lsem.at[3]),
    ]
    arrivals = [
        pltpu.make_async_copy(q_hbm, q_ref, asem.at[0]),
        pltpu.make_async_copy(plen_hbm, plen_ref, asem.at[1]),
        pltpu.make_async_copy(slen_hbm, slen_ref, asem.at[2]),
    ]
    for copy in arrivals:
        copy.start()
    for copy in locals_:
        copy.start()

    barrier = pltpu.get_barrier_semaphore()
    for x in range(1, samples):
        pl.semaphore_signal(barrier, inc=1, device_id=(row, peer(x)), device_id_type=MESH)
    pl.semaphore_signal(barrier, inc=1, device_id=(above, me), device_id_type=MESH)
    pl.semaphore_signal(barrier, inc=1, device_id=(below, me), device_id_type=MESH)

    padding = (TILE - steps) * KVH
    suf_raw[pl.ds((slots + steps) * KVH, padding)] = jnp.zeros((padding, 2, HEAD_SIZE), BF16)
    spare = sufs.shape[2] - slots
    sufs[:, :, pl.ds(slots, spare)] = jnp.zeros((KVH, 2, spare, HEAD_SIZE), BF16)
    order = permutation()
    for copy in arrivals:
        copy.wait()
    wide = q_ref[...].astype(F32)
    for g in range(KVH):
        parts = [
            wide[:, (g * group + x) * HEAD_SIZE : (g * group + x + 1) * HEAD_SIZE]
            for x in range(group)
        ]
        qall[0, g] = jnp.concatenate(parts, axis=0).astype(BF16)

    locals_[0].wait()
    take_apart(order, tail_raw, stage, 0, block // TILE)
    pl.semaphore_wait(barrier, samples + 1)

    def heads(c):
        return pl.ds(c * PAIR, PAIR)

    def remote(source, target, send, recv, device):
        return pltpu.make_async_remote_copy(
            src_ref=source, dst_ref=target, send_sem=send, recv_sem=recv,
            device_id=device, device_id_type=MESH,
        )

    def q_copy(x, c):
        i = place_of(x)
        return remote(
            qall.at[0, heads(c)], qall.at[i, heads(c)],
            qs_sem.at[i, c], qr_sem.at[i, c], (row, peer(x)),
        )

    def t_copy(c):
        return remote(
            stage.at[heads(c)], keys.at[heads(c), :, pl.ds(block, block)],
            ts_sem.at[c], tr_sem.at[c], (above, me),
        )

    def pair_sums(c):
        return remote(
            nbuf.at[c, pl.ds(half, half)], n1.at[c], p_sem.at[0, c], p_sem.at[1, c], (row, peer(1))
        )

    def pair_stats(c):
        return remote(sbuf.at[c], s1.at[c], p_sem.at[2, c], p_sem.at[3, c], (row, peer(1)))

    def far_sums(e, c):
        return remote(
            cbuf.at[c, e], n2.at[c, e], f_sem.at[0, e, c], f_sem.at[1, e, c], (row, peer(2 * e))
        )

    def far_stats(e, c):
        return remote(
            tbuf.at[c], s2.at[c, e], f_sem.at[2, e, c], f_sem.at[3, e, c], (row, peer(2 * e))
        )

    for c in range(chunks):
        for x in range(1, samples):
            q_copy(x, c).start()
        t_copy(c).start()
    for copy in locals_[1:]:
        copy.wait()
    take_apart(order, suf_raw, sufs, 0, slots // TILE + 1)

    shape = (rows, sufs.shape[2])
    place = lax.broadcasted_iota(jnp.int32, shape, 1)
    step = lax.rem(lax.broadcasted_iota(jnp.int32, shape, 0), steps)
    live = (place < slen_ref[0, 0]) | ((place >= slots) & (place - slots <= step))
    near_bias = jnp.where(live, 0.0, NEG).astype(F32)

    def near_chunk(c, carry):
        maxima, totals = [], []
        for i in range(PAIR):
            g = c * PAIR + i
            near[g], top, total = softmax_sums(qall[0, g], sufs[g, 0], sufs[g, 1], near_bias)
            maxima.append(top)
            totals.append(total)
        near_rows[c] = as_rows(maxima + totals)
        return carry

    lax.fori_loop(0, chunks, near_chunk, 0)

    take_apart(order, head_raw, keys, 0, block // TILE)
    place = lax.broadcasted_iota(jnp.int32, (1, 2 * block), 1)
    place = jnp.where(place < block, place + me * block, place + (samples + me - 1) * block)
    far_bias = jnp.where(place < plen_ref[row], 0.0, NEG).astype(F32)
    every = samples * rows

    def partial(c):
        for x in range(1, samples):
            q_copy(x, c).wait_recv()
        t_copy(c).wait_recv()
        maxima, totals = [], []
        for i in range(PAIR):
            g = c * PAIR + i
            queries = qall[:, g].reshape(every, HEAD_SIZE)
            numerator, top, total = softmax_sums(queries, keys[g, 0], keys[g, 1], far_bias)
            nbuf[c, :, i] = numerator.reshape(samples, rows, HEAD_SIZE)
            maxima.append(top)
            totals.append(total)
        pair_sums(c).start()
        sbuf[c] = as_rows(maxima + totals)
        pair_stats(c).start()

    def join_pair(c):
        pair_stats(c).wait_recv()
        tiles = [sbuf[c], pltpu.roll(s1[c], every // 2, 1)]
        peak, totals, factors = join_rows(tiles)
        rank = lax.broadcasted_iota(jnp.int32, peak.shape, 0)
        tbuf[c] = jnp.where(rank < PAIR, peak, totals)
        for e in range(1, half):
            far_stats(e, c).start()
        mine, other = as_columns(factors)
        pair_sums(c).wait_recv()
        for e in list(range(1, half)) + [0]:
            span = slice(e * rows, (e + 1) * rows)
            for i in range(PAIR):
                cbuf[c, e, i] = nbuf[c, e, i] * mine[i][span] + n1[c, e, i] * other[i][span]
            if e:
                far_sums(e, c).start()

    def finish(c):
        tiles = [near_rows[c], tbuf[c][:, :HEAD_SIZE]]
        for e in range(1, half):
            far_stats(e, c).wait_recv()
            tiles.append(pltpu.roll(s2[c, e], every - e * rows, 1)[:, :HEAD_SIZE])
        _, totals, factors = join_rows(tiles)
        totals = pltpu.roll(totals, 8 - PAIR, 0)
        columns = as_columns([f / totals for f in factors])
        for e in range(1, half):
            far_sums(e, c).wait_recv()
        for i in range(PAIR):
            g = c * PAIR + i
            result = near[g] * columns[0][i][:rows] + cbuf[c, 0, i] * columns[1][i][:rows]
            for e in range(1, half):
                result = result + n2[c, e, i] * columns[e + 1][i][:rows]
            flat = [result[x * steps : (x + 1) * steps] for x in range(group)]
            o_ref[:, g * group * HEAD_SIZE : (g + 1) * group * HEAD_SIZE] = jnp.concatenate(
                flat, axis=1
            ).astype(BF16)

    for c in range(chunks + 2):
        if c < chunks:
            partial(c)
        if 1 <= c <= chunks:
            join_pair(c - 1)
        if c >= 2:
            finish(c - 2)

    for c in range(chunks):
        t_copy(c).wait_send()
        pair_sums(c).wait_send()
        pair_stats(c).wait_send()
        for x in range(1, samples):
            q_copy(x, c).wait_send()
        for e in range(1, half):
            far_sums(e, c).wait_send()
            far_stats(e, c).wait_send()


def by_head(pairs):
    count = pairs.shape[0]
    split = pairs.reshape(count, 2, KVH, HEAD_SIZE).transpose(0, 2, 1, 3)
    return split.reshape(count * KVH, 2, HEAD_SIZE)


def per_device(queries, new_kv, suffix_kv, suffix_len, prefix_head, prefix_tail, prefix_len):
    samples = lax.axis_size("sample")
    prompts = lax.axis_size("prompt")
    steps, width = queries.shape[2:]
    group = width // (KVH * HEAD_SIZE)
    rows = steps * group
    block = prefix_head.shape[1]
    slots = suffix_kv.shape[2]
    chunks = KVH // PAIR
    half, every = samples // 2, samples * rows
    sem = pltpu.SemaphoreType.DMA
    attended = pl.pallas_call(
        functools.partial(kernel, samples, prompts),
        out_shape=jax.ShapeDtypeStruct((steps, width), BF16),
        in_specs=[pl.BlockSpec(memory_space=pl.ANY)] * 7,
        out_specs=pl.BlockSpec(memory_space=pltpu.VMEM),
        scratch_shapes=[
            pltpu.SMEM(prefix_len.shape, jnp.int32),
            pltpu.SMEM(suffix_len.shape, jnp.int32),
            pltpu.VMEM((steps, width), BF16),
            pltpu.VMEM((block * KVH, 2, HEAD_SIZE), BF16),
            pltpu.VMEM(((slots + TILE) * KVH, 2, HEAD_SIZE), BF16),
            pltpu.VMEM((block * KVH, 2, HEAD_SIZE), BF16),
            pltpu.VMEM((samples, KVH, rows, HEAD_SIZE), BF16),
            pltpu.VMEM((KVH, 2, 2 * block, HEAD_SIZE), BF16),
            pltpu.VMEM((KVH, 2, block, HEAD_SIZE), BF16),
            pltpu.VMEM((KVH, 2, slots + HEAD_SIZE, HEAD_SIZE), BF16),
            pltpu.VMEM((KVH, rows, HEAD_SIZE), F32),
            pltpu.VMEM((chunks, 8, HEAD_SIZE), F32),
            pltpu.VMEM((chunks, samples, PAIR, rows, HEAD_SIZE), F32),
            pltpu.VMEM((chunks, 8, every), F32),
            pltpu.VMEM((chunks, half, PAIR, rows, HEAD_SIZE), F32),
            pltpu.VMEM((chunks, 8, every), F32),
            pltpu.VMEM((chunks, half, PAIR, rows, HEAD_SIZE), F32),
            pltpu.VMEM((chunks, 8, every), F32),
            pltpu.VMEM((chunks, half, PAIR, rows, HEAD_SIZE), F32),
            pltpu.VMEM((chunks, half, 8, every), F32),
            sem((3,)), sem((4,)),
            sem((samples, chunks)), sem((samples, chunks)),
            sem((chunks,)), sem((chunks,)),
            sem((4, chunks)), sem((4, half, chunks)),
        ],
        compiler_params=pltpu.CompilerParams(
            collective_id=0, has_side_effects=True, vmem_limit_bytes=64 * 1024 * 1024
        ),
    )(
        prefix_len, suffix_len, queries[0, 0], by_head(new_kv[0, 0]), by_head(suffix_kv[0, 0]),
        by_head(prefix_head[0]), by_head(prefix_tail[0]),
    )
    return attended.reshape(queries.shape)


def solution(mesh):
    in_specs = (
        P("prompt", "sample", None, None),
        P("prompt", "sample", None, None, None),
        P("prompt", "sample", None, None, None),
        P("prompt", "sample"),
        P("prompt", "sample", None, None),
        P("prompt", "sample", None, None),
        P(),
    )
    out_specs = P("prompt", "sample", None, None)
    return jax.shard_map(
        per_device, mesh=mesh, in_specs=in_specs, out_specs=out_specs, check_vma=False
    )
```

```python
import functools

import jax
import jax.numpy as jnp
from jax import lax
from jax.experimental import pallas as pl
from jax.experimental.pallas import tpu as pltpu
from jax.sharding import PartitionSpec as P

KVH = 8
HEAD_SIZE = 128
NEG = -1e30
FLOOR = -1e29
PAIR = 2
FEW = 4
MESH = pl.DeviceIdType.MESH
F32 = jnp.float32
BF16 = jnp.bfloat16


def softmax_sums(queries, pairs, bias):
    contract = (((1,), (1,)), ((), ()))
    scores = [
        lax.dot_general(q, p, contract, preferred_element_type=F32) for q, p in zip(queries, pairs)
    ]
    masked = [s * HEAD_SIZE ** (-0.5) + bias for s in scores]
    maxima = [jnp.maximum(jnp.max(m, axis=1, keepdims=True), FLOOR) for m in masked]
    weights = [jnp.exp(m - top) for m, top in zip(masked, maxima)]
    totals = [jnp.sum(w, axis=1, keepdims=True) for w in weights]
    weights = [pltpu.roll(w, 1, 1) for w in weights]
    high = [w.astype(BF16) for w in weights]
    low = [(w - h.astype(F32)).astype(BF16) for w, h in zip(weights, high)]
    numerators = [
        jnp.dot(h, p, preferred_element_type=F32) + jnp.dot(l, p, preferred_element_type=F32)
        for h, l, p in zip(high, low, pairs)
    ]
    return numerators, maxima, totals


def put_stats(stats, lane, head, maxima, totals):
    return jnp.where(lane == head, maxima, jnp.where(lane == KVH + head, totals, stats))


def kernel(
    samples, prompts,
    plen_hbm, slen_hbm, q_hbm, new_ref, suf_ref, head_ref, tail_ref, o_ref,
    plen_ref, slen_ref, q_ref, qall, keys, stage, sufs, nsend, nrecv, ssend, srecv, near,
    asem, lsem, qs_sem, qr_sem, ts_sem, tr_sem, ns_sem, nr_sem, ss_sem, sr_sem,
):
    row, me = lax.axis_index("prompt"), lax.axis_index("sample")
    steps = q_ref.shape[0]
    group = q_ref.shape[1] // (KVH * HEAD_SIZE)
    rows = steps * group
    block = head_ref.shape[0]
    slots = suf_ref.shape[0]
    chunks = KVH // PAIR
    above = lax.rem(row + prompts - 1, prompts)
    below = lax.rem(row + 1, prompts)

    def lanes(g):
        return pl.ds(g * HEAD_SIZE, HEAD_SIZE)

    def local(kind, g):
        source = (tail_ref, suf_ref, new_ref, head_ref)[kind]
        target = (
            lambda: stage.at[g],
            lambda: sufs.at[g, pl.ds(0, slots)],
            lambda: sufs.at[g, pl.ds(slots, steps)],
            lambda: keys.at[g, pl.ds(0, block)],
        )[kind]
        return pltpu.make_async_copy(source.at[:, :, lanes(g)], target(), lsem.at[kind, g])

    arrivals = [
        pltpu.make_async_copy(q_hbm, q_ref, asem.at[0]),
        pltpu.make_async_copy(plen_hbm, plen_ref, asem.at[1]),
        pltpu.make_async_copy(slen_hbm, slen_ref, asem.at[2]),
    ]
    for copy in arrivals:
        copy.start()
    for g in range(KVH):
        local(0, g).start()

    barrier = pltpu.get_barrier_semaphore()
    for d in range(1, samples):
        pl.semaphore_signal(
            barrier, inc=1, device_id=(row, lax.rem(me + d, samples)), device_id_type=MESH
        )
    pl.semaphore_signal(barrier, inc=1, device_id=(above, me), device_id_type=MESH)
    pl.semaphore_signal(barrier, inc=1, device_id=(below, me), device_id_type=MESH)

    spare = sufs.shape[1] - slots
    for g in range(KVH):
        sufs[g, pl.ds(slots, spare)] = jnp.zeros((spare, 2, HEAD_SIZE), BF16)
    for g in range(KVH):
        for kind in range(1, 4):
            local(kind, g).start()

    for copy in arrivals:
        copy.wait()
    wide = q_ref[...].astype(F32)
    for g in range(KVH):
        parts = [
            wide[:, (g * group + x) * HEAD_SIZE : (g * group + x + 1) * HEAD_SIZE]
            for x in range(group)
        ]
        qall[0, g] = jnp.concatenate(parts, axis=0).astype(BF16)

    pl.semaphore_wait(barrier, samples + 1)

    def heads(c):
        return pl.ds(c * PAIR, PAIR)

    def q_copy(d, c):
        return pltpu.make_async_remote_copy(
            src_ref=qall.at[0, heads(c)], dst_ref=qall.at[d, heads(c)],
            send_sem=qs_sem.at[d, c], recv_sem=qr_sem.at[d, c],
            device_id=(row, lax.rem(me + d, samples)), device_id_type=MESH,
        )

    def t_copy(c):
        return pltpu.make_async_remote_copy(
            src_ref=stage.at[heads(c)], dst_ref=keys.at[heads(c), pl.ds(block, block)],
            send_sem=ts_sem.at[c], recv_sem=tr_sem.at[c],
            device_id=(above, me), device_id_type=MESH,
        )

    def n_copy(d, c):
        return pltpu.make_async_remote_copy(
            src_ref=nsend.at[d, heads(c)], dst_ref=nrecv.at[d, heads(c)],
            send_sem=ns_sem.at[d, c], recv_sem=nr_sem.at[d, c],
            device_id=(row, lax.rem(me + samples - d, samples)), device_id_type=MESH,
        )

    def s_copy(d):
        return pltpu.make_async_remote_copy(
            src_ref=ssend, dst_ref=srecv.at[d],
            send_sem=ss_sem.at[d], recv_sem=sr_sem.at[d],
            device_id=(row, lax.rem(me + samples - d, samples)), device_id_type=MESH,
        )

    for c in range(chunks):
        for d in range(1, samples):
            q_copy(d, c).start()
    for c in range(chunks):
        for g in range(c * PAIR, (c + 1) * PAIR):
            local(0, g).wait()
        t_copy(c).start()

    shape = (rows, 2 * sufs.shape[1])
    column = lax.broadcasted_iota(jnp.int32, shape, 1)
    step = lax.rem(lax.broadcasted_iota(jnp.int32, shape, 0), steps)
    place = column // 2
    live = (place < slen_ref[0, 0]) | ((place >= slots) & (place - slots <= step))
    near_bias = jnp.where(live & (lax.rem(column, 2) == 0), 0.0, NEG).astype(F32)
    lane = lax.broadcasted_iota(jnp.int32, (rows, HEAD_SIZE), 1)

    def near_heads(k, stats):
        group_heads = [k * FEW + i for i in range(FEW)]
        for g in group_heads:
            for kind in range(1, 3):
                local(kind, g).wait()
        pairs = [sufs.at[g].reshape(2 * sufs.shape[1], HEAD_SIZE)[...] for g in group_heads]
        sums = softmax_sums([qall[0, g] for g in group_heads], pairs, near_bias)
        for g, numerator, maxima, totals in zip(group_heads, *sums):
            near[g] = numerator
            stats = put_stats(stats, lane, g, maxima, totals)
        return stats

    near_stats = lax.fori_loop(0, KVH // FEW, near_heads, jnp.zeros((rows, HEAD_SIZE), F32))
    padding = jnp.zeros((HEAD_SIZE - rows, HEAD_SIZE), F32)
    near_stats = jnp.concatenate([near_stats, padding], axis=0).T[: 2 * KVH]

    column = lax.broadcasted_iota(jnp.int32, (1, 4 * block), 1)
    place = column // 2
    place = jnp.where(place < block, place + me * block, place + (samples + me - 1) * block)
    far_bias = jnp.where((place < plen_ref[row]) & (lax.rem(column, 2) == 0), 0.0, NEG).astype(F32)
    every = samples * rows
    far_lane = lax.broadcasted_iota(jnp.int32, (every, HEAD_SIZE), 1)

    def far_chunk(c, stats):
        for d in range(1, samples):
            q_copy(d, c).wait_recv()
        t_copy(c).wait_recv()
        both = [c * PAIR + i for i in range(PAIR)]
        for g in both:
            local(3, g).wait()
        pairs = [keys.at[g].reshape(4 * block, HEAD_SIZE)[...] for g in both]
        queries = [qall[:, g].reshape(every, HEAD_SIZE) for g in both]
        sums = softmax_sums(queries, pairs, far_bias)
        for g, numerator, maxima, totals in zip(both, *sums):
            nsend[:, g] = numerator.reshape(samples, rows, HEAD_SIZE)
            stats = put_stats(stats, far_lane, g, maxima, totals)
        for d in range(1, samples):
            n_copy(d, c).start()
        return stats

    far_stats = lax.fori_loop(0, chunks, far_chunk, jnp.full((every, HEAD_SIZE), 0.0, F32))
    ssend[...] = far_stats.T[: 2 * KVH]
    for d in range(1, samples):
        s_copy(d).start()
    for d in range(1, samples):
        s_copy(d).wait_recv()

    stats = [near_stats, ssend[:, :HEAD_SIZE]]
    for d in range(1, samples):
        stats.append(pltpu.roll(srecv[d], every - d * rows, 1)[:, :HEAD_SIZE])
    peak = functools.reduce(jnp.maximum, [s[:KVH] for s in stats])
    factors = [jnp.exp(s[:KVH] - peak) for s in stats]
    total = sum(s[KVH:] * f for s, f in zip(stats, factors))
    factors = [f / total for f in factors]
    factors = jnp.concatenate(factors, axis=0).T[:rows]

    def factor(k, g):
        return factors[:, k * KVH + g : k * KVH + g + 1]

    for c in range(chunks):
        for d in range(1, samples):
            n_copy(d, c).wait_recv()
        for g in range(c * PAIR, (c + 1) * PAIR):
            result = near[g] * factor(0, g) + nsend[0, g] * factor(1, g)
            for d in range(1, samples):
                result = result + nrecv[d, g] * factor(d + 1, g)
            o_ref[g] = result.astype(BF16)

    for c in range(chunks):
        t_copy(c).wait_send()
        for d in range(1, samples):
            q_copy(d, c).wait_send()
            n_copy(d, c).wait_send()
    for d in range(1, samples):
        s_copy(d).wait_send()


def per_device(queries, new_kv, suffix_kv, suffix_len, prefix_head, prefix_tail, prefix_len):
    samples = lax.axis_size("sample")
    prompts = lax.axis_size("prompt")
    steps, width = queries.shape[2:]
    group = width // (KVH * HEAD_SIZE)
    rows = steps * group
    block = prefix_head.shape[1]
    slots = suffix_kv.shape[2]
    chunks = KVH // PAIR
    near_len = slots + HEAD_SIZE // 2
    sem = pltpu.SemaphoreType.DMA
    attended = pl.pallas_call(
        functools.partial(kernel, samples, prompts),
        out_shape=jax.ShapeDtypeStruct((KVH, rows, HEAD_SIZE), BF16),
        in_specs=[pl.BlockSpec(memory_space=pl.ANY)] * 7,
        out_specs=pl.BlockSpec(memory_space=pltpu.VMEM),
        scratch_shapes=[
            pltpu.SMEM(prefix_len.shape, jnp.int32),
            pltpu.SMEM(suffix_len.shape, jnp.int32),
            pltpu.VMEM((steps, width), BF16),
            pltpu.VMEM((samples, KVH, rows, HEAD_SIZE), BF16),
            pltpu.VMEM((KVH, 2 * block, 2, HEAD_SIZE), BF16),
            pltpu.VMEM((KVH, block, 2, HEAD_SIZE), BF16),
            pltpu.VMEM((KVH, near_len, 2, HEAD_SIZE), BF16),
            pltpu.VMEM((samples, KVH, rows, HEAD_SIZE), F32),
            pltpu.VMEM((samples, KVH, rows, HEAD_SIZE), F32),
            pltpu.VMEM((2 * KVH, samples * rows), F32),
            pltpu.VMEM((samples, 2 * KVH, samples * rows), F32),
            pltpu.VMEM((KVH, rows, HEAD_SIZE), F32),
            sem((3,)), sem((4, KVH)),
            sem((samples, chunks)), sem((samples, chunks)),
            sem((chunks,)), sem((chunks,)),
            sem((samples, chunks)), sem((samples, chunks)),
            sem((samples,)), sem((samples,)),
        ],
        compiler_params=pltpu.CompilerParams(
            collective_id=0, has_side_effects=True, vmem_limit_bytes=64 * 1024 * 1024
        ),
    )(
        prefix_len, suffix_len, queries[0, 0], new_kv[0, 0], suffix_kv[0, 0],
        prefix_head[0], prefix_tail[0],
    )
    attended = attended.reshape(KVH, group, steps, HEAD_SIZE).transpose(2, 0, 1, 3)
    return attended.reshape(queries.shape)


def solution(mesh):
    in_specs = (
        P("prompt", "sample", None, None),
        P("prompt", "sample", None, None, None),
        P("prompt", "sample", None, None, None),
        P("prompt", "sample"),
        P("prompt", "sample", None, None),
        P("prompt", "sample", None, None),
        P(),
    )
    out_specs = P("prompt", "sample", None, None)
    return jax.shard_map(
        per_device, mesh=mesh, in_specs=in_specs, out_specs=out_specs, check_vma=False
    )
```

```python
import functools

import jax
import jax.numpy as jnp
from jax import lax
from jax.experimental import pallas as pl
from jax.experimental.pallas import tpu as pltpu
from jax.sharding import PartitionSpec as P

KVH = 8
HEAD_SIZE = 128
NEG = -1e30
FLOOR = -1e29
PAIR = 2
FEW = 4
MESH = pl.DeviceIdType.MESH
F32 = jnp.float32
BF16 = jnp.bfloat16


def softmax_sums(queries, pairs, bias):
    contract = (((1,), (1,)), ((), ()))
    scores = [
        lax.dot_general(q, p, contract, preferred_element_type=F32) for q, p in zip(queries, pairs)
    ]
    masked = [s * HEAD_SIZE ** (-0.5) + bias for s in scores]
    maxima = [jnp.maximum(jnp.max(m, axis=1, keepdims=True), FLOOR) for m in masked]
    weights = [jnp.exp(m - top) for m, top in zip(masked, maxima)]
    totals = [jnp.sum(w, axis=1, keepdims=True) for w in weights]
    weights = [pltpu.roll(w, 1, 1) for w in weights]
    high = [w.astype(BF16) for w in weights]
    low = [(w - h.astype(F32)).astype(BF16) for w, h in zip(weights, high)]
    numerators = [
        jnp.dot(h, p, preferred_element_type=F32) + jnp.dot(l, p, preferred_element_type=F32)
        for h, l, p in zip(high, low, pairs)
    ]
    return numerators, maxima, totals


def put_stats(stats, lane, head, maxima, totals):
    return jnp.where(lane == head, maxima, jnp.where(lane == KVH + head, totals, stats))


def kernel(
    samples, prompts,
    plen_hbm, slen_hbm, q_hbm, new_ref, suf_ref, head_ref, tail_ref, o_ref,
    plen_ref, slen_ref, q_ref, qall, keys, stage, sufs, nsend, nrecv, ssend, srecv, near,
    asem, lsem, qs_sem, qr_sem, ts_sem, tr_sem, ns_sem, nr_sem, ss_sem, sr_sem,
):
    row, me = lax.axis_index("prompt"), lax.axis_index("sample")
    steps = q_ref.shape[0]
    group = q_ref.shape[1] // (KVH * HEAD_SIZE)
    rows = steps * group
    block = head_ref.shape[0]
    slots = suf_ref.shape[0]
    chunks = KVH // PAIR
    above = lax.rem(row + prompts - 1, prompts)
    below = lax.rem(row + 1, prompts)

    def peer(x):
        other, bit = 0, 1
        while bit < samples:
            digit = lax.rem(me // bit, 2)
            other = other + bit * (1 - digit if x & bit else digit)
            bit *= 2
        return (row, other)

    def lanes(g):
        return pl.ds(g * HEAD_SIZE, HEAD_SIZE)

    def local(kind, g):
        source = (tail_ref, suf_ref, new_ref, head_ref)[kind]
        target = (
            lambda: stage.at[g],
            lambda: sufs.at[g, pl.ds(0, slots)],
            lambda: sufs.at[g, pl.ds(slots, steps)],
            lambda: keys.at[g, pl.ds(0, block)],
        )[kind]
        return pltpu.make_async_copy(source.at[:, :, lanes(g)], target(), lsem.at[kind, g])

    arrivals = [
        pltpu.make_async_copy(q_hbm, q_ref, asem.at[0]),
        pltpu.make_async_copy(plen_hbm, plen_ref, asem.at[1]),
        pltpu.make_async_copy(slen_hbm, slen_ref, asem.at[2]),
    ]
    for copy in arrivals:
        copy.start()
    for g in range(KVH):
        local(0, g).start()

    barrier = pltpu.get_barrier_semaphore()
    for d in range(1, samples):
        pl.semaphore_signal(barrier, inc=1, device_id=peer(d), device_id_type=MESH)
    pl.semaphore_signal(barrier, inc=1, device_id=(above, me), device_id_type=MESH)
    pl.semaphore_signal(barrier, inc=1, device_id=(below, me), device_id_type=MESH)

    spare = sufs.shape[1] - slots
    for g in range(KVH):
        sufs[g, pl.ds(slots, spare)] = jnp.zeros((spare, 2, HEAD_SIZE), BF16)
    for g in range(KVH):
        for kind in range(1, 4):
            local(kind, g).start()

    for copy in arrivals:
        copy.wait()
    wide = q_ref[...].astype(F32)
    for g in range(KVH):
        parts = [
            wide[:, (g * group + x) * HEAD_SIZE : (g * group + x + 1) * HEAD_SIZE]
            for x in range(group)
        ]
        qall[0, g] = jnp.concatenate(parts, axis=0).astype(BF16)

    pl.semaphore_wait(barrier, samples + 1)

    def heads(c):
        return pl.ds(c * PAIR, PAIR)

    def q_copy(d, c):
        onward = d % 2 == 1 and d > 1
        return pltpu.make_async_remote_copy(
            src_ref=qall.at[d - 1 if onward else 0, heads(c)], dst_ref=qall.at[d, heads(c)],
            send_sem=qs_sem.at[d, c], recv_sem=qr_sem.at[d, c],
            device_id=peer(1 if onward else d), device_id_type=MESH,
        )

    def t_copy(c):
        return pltpu.make_async_remote_copy(
            src_ref=stage.at[heads(c)], dst_ref=keys.at[heads(c), pl.ds(block, block)],
            send_sem=ts_sem.at[c], recv_sem=tr_sem.at[c],
            device_id=(above, me), device_id_type=MESH,
        )

    def n_copy(d, c):
        return pltpu.make_async_remote_copy(
            src_ref=nsend.at[d, heads(c)], dst_ref=nrecv.at[d, heads(c)],
            send_sem=ns_sem.at[d, c], recv_sem=nr_sem.at[d, c],
            device_id=peer(d), device_id_type=MESH,
        )

    def s_copy(d):
        return pltpu.make_async_remote_copy(
            src_ref=ssend, dst_ref=srecv.at[d],
            send_sem=ss_sem.at[d], recv_sem=sr_sem.at[d],
            device_id=peer(d), device_id_type=MESH,
        )

    for c in range(chunks):
        for d in [1] + list(range(2, samples, 2)):
            q_copy(d, c).start()
    for c in range(chunks):
        for g in range(c * PAIR, (c + 1) * PAIR):
            local(0, g).wait()
        t_copy(c).start()

    shape = (rows, 2 * sufs.shape[1])
    column = lax.broadcasted_iota(jnp.int32, shape, 1)
    step = lax.rem(lax.broadcasted_iota(jnp.int32, shape, 0), steps)
    place = column // 2
    live = (place < slen_ref[0, 0]) | ((place >= slots) & (place - slots <= step))
    near_bias = jnp.where(live & (lax.rem(column, 2) == 0), 0.0, NEG).astype(F32)
    lane = lax.broadcasted_iota(jnp.int32, (rows, HEAD_SIZE), 1)

    def near_heads(k, stats):
        group_heads = [k * FEW + i for i in range(FEW)]
        for g in group_heads:
            for kind in range(1, 3):
                local(kind, g).wait()
        pairs = [sufs.at[g].reshape(2 * sufs.shape[1], HEAD_SIZE)[...] for g in group_heads]
        sums = softmax_sums([qall[0, g] for g in group_heads], pairs, near_bias)
        for g, numerator, maxima, totals in zip(group_heads, *sums):
            near[g] = numerator
            stats = put_stats(stats, lane, g, maxima, totals)
        return stats

    def pass_on(c):
        for d in range(2, samples, 2):
            q_copy(d, c).wait_recv()
            q_copy(d + 1, c).start()

    near_stats = jnp.zeros((rows, HEAD_SIZE), F32)
    for k in range(KVH // FEW):
        near_stats = near_heads(k, near_stats)
        for c in range(k * FEW // PAIR, (k + 1) * FEW // PAIR):
            pass_on(c)
    padding = jnp.zeros((HEAD_SIZE - rows, HEAD_SIZE), F32)
    near_stats = jnp.concatenate([near_stats, padding], axis=0).T[: 2 * KVH]

    column = lax.broadcasted_iota(jnp.int32, (1, 4 * block), 1)
    place = column // 2
    place = jnp.where(place < block, place + me * block, place + (samples + me - 1) * block)
    far_bias = jnp.where((place < plen_ref[row]) & (lax.rem(column, 2) == 0), 0.0, NEG).astype(F32)
    every = samples * rows
    far_lane = lax.broadcasted_iota(jnp.int32, (every, HEAD_SIZE), 1)

    def far_chunk(c, stats):
        for d in range(1, samples, 2):
            q_copy(d, c).wait_recv()
        t_copy(c).wait_recv()
        both = [c * PAIR + i for i in range(PAIR)]
        for g in both:
            local(3, g).wait()
        pairs = [keys.at[g].reshape(4 * block, HEAD_SIZE)[...] for g in both]
        queries = [qall[:, g].reshape(every, HEAD_SIZE) for g in both]
        sums = softmax_sums(queries, pairs, far_bias)
        for g, numerator, maxima, totals in zip(both, *sums):
            nsend[:, g] = numerator.reshape(samples, rows, HEAD_SIZE)
            stats = put_stats(stats, far_lane, g, maxima, totals)
        for d in range(1, samples):
            n_copy(d, c).start()
        return stats

    far_stats = lax.fori_loop(0, chunks, far_chunk, jnp.full((every, HEAD_SIZE), 0.0, F32))
    ssend[...] = far_stats.T[: 2 * KVH]
    for d in range(1, samples):
        s_copy(d).start()
    for d in range(1, samples):
        s_copy(d).wait_recv()

    stats = [near_stats, ssend[:, :HEAD_SIZE]]
    for d in range(1, samples):
        stats.append(pltpu.roll(srecv[d], every - d * rows, 1)[:, :HEAD_SIZE])
    peak = functools.reduce(jnp.maximum, [s[:KVH] for s in stats])
    factors = [jnp.exp(s[:KVH] - peak) for s in stats]
    total = sum(s[KVH:] * f for s, f in zip(stats, factors))
    factors = [f / total for f in factors]
    factors = jnp.concatenate(factors, axis=0).T[:rows]

    def factor(k, g):
        return factors[:, k * KVH + g : k * KVH + g + 1]

    for c in range(chunks):
        for d in range(1, samples):
            n_copy(d, c).wait_recv()
        for g in range(c * PAIR, (c + 1) * PAIR):
            result = near[g] * factor(0, g) + nsend[0, g] * factor(1, g)
            for d in range(1, samples):
                result = result + nrecv[d, g] * factor(d + 1, g)
            o_ref[g] = result.astype(BF16)

    for c in range(chunks):
        t_copy(c).wait_send()
        for d in range(1, samples):
            q_copy(d, c).wait_send()
            n_copy(d, c).wait_send()
    for d in range(1, samples):
        s_copy(d).wait_send()


def per_device(queries, new_kv, suffix_kv, suffix_len, prefix_head, prefix_tail, prefix_len):
    samples = lax.axis_size("sample")
    prompts = lax.axis_size("prompt")
    steps, width = queries.shape[2:]
    group = width // (KVH * HEAD_SIZE)
    rows = steps * group
    block = prefix_head.shape[1]
    slots = suffix_kv.shape[2]
    chunks = KVH // PAIR
    near_len = slots + HEAD_SIZE // 2
    sem = pltpu.SemaphoreType.DMA
    attended = pl.pallas_call(
        functools.partial(kernel, samples, prompts),
        out_shape=jax.ShapeDtypeStruct((KVH, rows, HEAD_SIZE), BF16),
        in_specs=[pl.BlockSpec(memory_space=pl.ANY)] * 7,
        out_specs=pl.BlockSpec(memory_space=pltpu.VMEM),
        scratch_shapes=[
            pltpu.SMEM(prefix_len.shape, jnp.int32),
            pltpu.SMEM(suffix_len.shape, jnp.int32),
            pltpu.VMEM((steps, width), BF16),
            pltpu.VMEM((samples, KVH, rows, HEAD_SIZE), BF16),
            pltpu.VMEM((KVH, 2 * block, 2, HEAD_SIZE), BF16),
            pltpu.VMEM((KVH, block, 2, HEAD_SIZE), BF16),
            pltpu.VMEM((KVH, near_len, 2, HEAD_SIZE), BF16),
            pltpu.VMEM((samples, KVH, rows, HEAD_SIZE), F32),
            pltpu.VMEM((samples, KVH, rows, HEAD_SIZE), F32),
            pltpu.VMEM((2 * KVH, samples * rows), F32),
            pltpu.VMEM((samples, 2 * KVH, samples * rows), F32),
            pltpu.VMEM((KVH, rows, HEAD_SIZE), F32),
            sem((3,)), sem((4, KVH)),
            sem((samples, chunks)), sem((samples, chunks)),
            sem((chunks,)), sem((chunks,)),
            sem((samples, chunks)), sem((samples, chunks)),
            sem((samples,)), sem((samples,)),
        ],
        compiler_params=pltpu.CompilerParams(
            collective_id=0, has_side_effects=True, vmem_limit_bytes=64 * 1024 * 1024
        ),
    )(
        prefix_len, suffix_len, queries[0, 0], new_kv[0, 0], suffix_kv[0, 0],
        prefix_head[0], prefix_tail[0],
    )
    attended = attended.reshape(KVH, group, steps, HEAD_SIZE).transpose(2, 0, 1, 3)
    return attended.reshape(queries.shape)


def solution(mesh):
    in_specs = (
        P("prompt", "sample", None, None),
        P("prompt", "sample", None, None, None),
        P("prompt", "sample", None, None, None),
        P("prompt", "sample"),
        P("prompt", "sample", None, None),
        P("prompt", "sample", None, None),
        P(),
    )
    out_specs = P("prompt", "sample", None, None)
    return jax.shard_map(
        per_device, mesh=mesh, in_specs=in_specs, out_specs=out_specs, check_vma=False
    )
```

```python
import functools
import math

import jax
import jax.numpy as jnp
from jax import lax
from jax.experimental import pallas as pl
from jax.experimental.pallas import tpu as pltpu
from jax.sharding import PartitionSpec as P

KVH = 8
HEAD_SIZE = 128
NEG = -1e30
SCALE = math.log2(math.e) * HEAD_SIZE ** (-0.5)
FLOOR = -1e29
PAIR = 2
FEW = 4
MESH = pl.DeviceIdType.MESH
F32 = jnp.float32
BF16 = jnp.bfloat16


def softmax_sums(queries, pairs, bias):
    contract = (((1,), (1,)), ((), ()))
    scores = [
        lax.dot_general(q, p, contract, preferred_element_type=F32) for q, p in zip(queries, pairs)
    ]
    masked = [s * SCALE + bias for s in scores]
    maxima = [jnp.maximum(jnp.max(m, axis=1, keepdims=True), FLOOR) for m in masked]
    weights = [jnp.exp2(m - top) for m, top in zip(masked, maxima)]
    totals = [jnp.sum(w, axis=1, keepdims=True) for w in weights]
    weights = [pltpu.roll(w, 1, 1) for w in weights]
    high = [w.astype(BF16) for w in weights]
    low = [(w - h.astype(F32)).astype(BF16) for w, h in zip(weights, high)]
    numerators = [
        jnp.dot(h, p, preferred_element_type=F32) + jnp.dot(l, p, preferred_element_type=F32)
        for h, l, p in zip(high, low, pairs)
    ]
    return numerators, maxima, totals


def put_stats(stats, lane, head, maxima, totals):
    return jnp.where(lane == head, maxima, jnp.where(lane == KVH + head, totals, stats))


def kernel(
    samples, prompts,
    plen_hbm, slen_hbm, q_hbm, new_ref, suf_ref, head_ref, tail_ref, o_ref,
    plen_ref, slen_ref, q_ref, qall, keys, stage, sufs, nsend, nrecv, ssend, srecv, near,
    asem, lsem, qs_sem, qr_sem, ts_sem, tr_sem, ns_sem, nr_sem, ss_sem, sr_sem,
):
    row, me = lax.axis_index("prompt"), lax.axis_index("sample")
    steps = q_ref.shape[0]
    group = q_ref.shape[1] // (KVH * HEAD_SIZE)
    rows = steps * group
    block = head_ref.shape[0]
    slots = suf_ref.shape[0]
    chunks = KVH // PAIR
    above = lax.rem(row + prompts - 1, prompts)
    below = lax.rem(row + 1, prompts)

    def lanes(g):
        return pl.ds(g * HEAD_SIZE, HEAD_SIZE)

    def local(kind, g):
        source = (tail_ref, suf_ref, new_ref, head_ref)[kind]
        target = (
            lambda: stage.at[g],
            lambda: sufs.at[g, pl.ds(0, slots)],
            lambda: sufs.at[g, pl.ds(slots, steps)],
            lambda: keys.at[g, pl.ds(0, block)],
        )[kind]
        return pltpu.make_async_copy(source.at[:, :, lanes(g)], target(), lsem.at[kind, g])

    arrivals = [
        pltpu.make_async_copy(q_hbm, q_ref, asem.at[0]),
        pltpu.make_async_copy(plen_hbm, plen_ref, asem.at[1]),
        pltpu.make_async_copy(slen_hbm, slen_ref, asem.at[2]),
    ]
    for copy in arrivals:
        copy.start()
    for g in range(KVH):
        local(0, g).start()

    barrier = pltpu.get_barrier_semaphore()
    for d in range(1, samples):
        pl.semaphore_signal(
            barrier, inc=1, device_id=(row, lax.rem(me + d, samples)), device_id_type=MESH
        )
    pl.semaphore_signal(barrier, inc=1, device_id=(above, me), device_id_type=MESH)
    pl.semaphore_signal(barrier, inc=1, device_id=(below, me), device_id_type=MESH)

    spare = sufs.shape[1] - slots
    for g in range(KVH):
        sufs[g, pl.ds(slots, spare)] = jnp.zeros((spare, 2, HEAD_SIZE), BF16)
    for g in range(KVH):
        for kind in range(1, 4):
            local(kind, g).start()

    for copy in arrivals:
        copy.wait()
    wide = q_ref[...].astype(F32)
    for g in range(KVH):
        parts = [
            wide[:, (g * group + x) * HEAD_SIZE : (g * group + x + 1) * HEAD_SIZE]
            for x in range(group)
        ]
        qall[0, g] = jnp.concatenate(parts, axis=0).astype(BF16)

    pl.semaphore_wait(barrier, samples + 1)

    def heads(c):
        return pl.ds(c * PAIR, PAIR)

    def q_copy(d, c):
        return pltpu.make_async_remote_copy(
            src_ref=qall.at[0, heads(c)], dst_ref=qall.at[d, heads(c)],
            send_sem=qs_sem.at[d, c], recv_sem=qr_sem.at[d, c],
            device_id=(row, lax.rem(me + d, samples)), device_id_type=MESH,
        )

    def t_copy(c):
        return pltpu.make_async_remote_copy(
            src_ref=stage.at[heads(c)], dst_ref=keys.at[heads(c), pl.ds(block, block)],
            send_sem=ts_sem.at[c], recv_sem=tr_sem.at[c],
            device_id=(above, me), device_id_type=MESH,
        )

    def n_copy(d, c):
        return pltpu.make_async_remote_copy(
            src_ref=nsend.at[d, heads(c)], dst_ref=nrecv.at[d, heads(c)],
            send_sem=ns_sem.at[d, c], recv_sem=nr_sem.at[d, c],
            device_id=(row, lax.rem(me + samples - d, samples)), device_id_type=MESH,
        )

    def s_copy(d):
        return pltpu.make_async_remote_copy(
            src_ref=ssend, dst_ref=srecv.at[d],
            send_sem=ss_sem.at[d], recv_sem=sr_sem.at[d],
            device_id=(row, lax.rem(me + samples - d, samples)), device_id_type=MESH,
        )

    for c in range(chunks):
        for d in range(1, samples):
            q_copy(d, c).start()
    for c in range(chunks):
        for g in range(c * PAIR, (c + 1) * PAIR):
            local(0, g).wait()
        t_copy(c).start()

    shape = (rows, 2 * sufs.shape[1])
    column = lax.broadcasted_iota(jnp.int32, shape, 1)
    step = lax.rem(lax.broadcasted_iota(jnp.int32, shape, 0), steps)
    place = column // 2
    live = (place < slen_ref[0, 0]) | ((place >= slots) & (place - slots <= step))
    near_bias = jnp.where(live & (lax.rem(column, 2) == 0), 0.0, NEG).astype(F32)
    lane = lax.broadcasted_iota(jnp.int32, (rows, HEAD_SIZE), 1)

    def near_heads(k, stats):
        group_heads = [k * FEW + i for i in range(FEW)]
        for g in group_heads:
            for kind in range(1, 3):
                local(kind, g).wait()
        pairs = [sufs.at[g].reshape(2 * sufs.shape[1], HEAD_SIZE)[...] for g in group_heads]
        sums = softmax_sums([qall[0, g] for g in group_heads], pairs, near_bias)
        for g, numerator, maxima, totals in zip(group_heads, *sums):
            near[g] = numerator
            stats = put_stats(stats, lane, g, maxima, totals)
        return stats

    near_stats = near_heads(0, jnp.zeros((rows, HEAD_SIZE), F32))

    column = lax.broadcasted_iota(jnp.int32, (1, 4 * block), 1)
    place = column // 2
    place = jnp.where(place < block, place + me * block, place + (samples + me - 1) * block)
    far_bias = jnp.where((place < plen_ref[row]) & (lax.rem(column, 2) == 0), 0.0, NEG).astype(F32)
    every = samples * rows
    far_lane = lax.broadcasted_iota(jnp.int32, (every, HEAD_SIZE), 1)

    def far_chunk(c, stats):
        for d in range(1, samples):
            q_copy(d, c).wait_recv()
        t_copy(c).wait_recv()
        both = [c * PAIR + i for i in range(PAIR)]
        for g in both:
            local(3, g).wait()
        pairs = [keys.at[g].reshape(4 * block, HEAD_SIZE)[...] for g in both]
        queries = [qall[:, g].reshape(every, HEAD_SIZE) for g in both]
        sums = softmax_sums(queries, pairs, far_bias)
        for g, numerator, maxima, totals in zip(both, *sums):
            nsend[:, g] = numerator.reshape(samples, rows, HEAD_SIZE)
            stats = put_stats(stats, far_lane, g, maxima, totals)
        for d in range(1, samples):
            n_copy(d, c).start()
        return stats

    far_stats = lax.fori_loop(0, chunks, far_chunk, jnp.full((every, HEAD_SIZE), 0.0, F32))
    ssend[...] = far_stats.T[: 2 * KVH]
    for d in range(1, samples):
        s_copy(d).start()
    for k in range(1, KVH // FEW):
        near_stats = near_heads(k, near_stats)
    padding = jnp.zeros((HEAD_SIZE - rows, HEAD_SIZE), F32)
    near_stats = jnp.concatenate([near_stats, padding], axis=0).T[: 2 * KVH]
    for d in range(1, samples):
        s_copy(d).wait_recv()

    stats = [near_stats, ssend[:, :HEAD_SIZE]]
    for d in range(1, samples):
        stats.append(pltpu.roll(srecv[d], every - d * rows, 1)[:, :HEAD_SIZE])
    peak = functools.reduce(jnp.maximum, [s[:KVH] for s in stats])
    factors = [jnp.exp2(s[:KVH] - peak) for s in stats]
    total = sum(s[KVH:] * f for s, f in zip(stats, factors))
    factors = [f / total for f in factors]
    factors = jnp.concatenate(factors, axis=0).T[:rows]

    def factor(k, g):
        return factors[:, k * KVH + g : k * KVH + g + 1]

    for c in range(chunks):
        for d in range(1, samples):
            n_copy(d, c).wait_recv()
        for g in range(c * PAIR, (c + 1) * PAIR):
            result = near[g] * factor(0, g) + nsend[0, g] * factor(1, g)
            for d in range(1, samples):
                result = result + nrecv[d, g] * factor(d + 1, g)
            o_ref[g] = result.astype(BF16)

    for c in range(chunks):
        t_copy(c).wait_send()
        for d in range(1, samples):
            q_copy(d, c).wait_send()
            n_copy(d, c).wait_send()
    for d in range(1, samples):
        s_copy(d).wait_send()


def per_device(queries, new_kv, suffix_kv, suffix_len, prefix_head, prefix_tail, prefix_len):
    samples = lax.axis_size("sample")
    prompts = lax.axis_size("prompt")
    steps, width = queries.shape[2:]
    group = width // (KVH * HEAD_SIZE)
    rows = steps * group
    block = prefix_head.shape[1]
    slots = suffix_kv.shape[2]
    chunks = KVH // PAIR
    near_len = slots + HEAD_SIZE // 2
    sem = pltpu.SemaphoreType.DMA
    attended = pl.pallas_call(
        functools.partial(kernel, samples, prompts),
        out_shape=jax.ShapeDtypeStruct((KVH, rows, HEAD_SIZE), BF16),
        in_specs=[pl.BlockSpec(memory_space=pl.ANY)] * 7,
        out_specs=pl.BlockSpec(memory_space=pltpu.VMEM),
        scratch_shapes=[
            pltpu.SMEM(prefix_len.shape, jnp.int32),
            pltpu.SMEM(suffix_len.shape, jnp.int32),
            pltpu.VMEM((steps, width), BF16),
            pltpu.VMEM((samples, KVH, rows, HEAD_SIZE), BF16),
            pltpu.VMEM((KVH, 2 * block, 2, HEAD_SIZE), BF16),
            pltpu.VMEM((KVH, block, 2, HEAD_SIZE), BF16),
            pltpu.VMEM((KVH, near_len, 2, HEAD_SIZE), BF16),
            pltpu.VMEM((samples, KVH, rows, HEAD_SIZE), F32),
            pltpu.VMEM((samples, KVH, rows, HEAD_SIZE), F32),
            pltpu.VMEM((2 * KVH, samples * rows), F32),
            pltpu.VMEM((samples, 2 * KVH, samples * rows), F32),
            pltpu.VMEM((KVH, rows, HEAD_SIZE), F32),
            sem((3,)), sem((4, KVH)),
            sem((samples, chunks)), sem((samples, chunks)),
            sem((chunks,)), sem((chunks,)),
            sem((samples, chunks)), sem((samples, chunks)),
            sem((samples,)), sem((samples,)),
        ],
        compiler_params=pltpu.CompilerParams(
            collective_id=0, has_side_effects=True, vmem_limit_bytes=64 * 1024 * 1024
        ),
    )(
        prefix_len, suffix_len, queries[0, 0], new_kv[0, 0], suffix_kv[0, 0],
        prefix_head[0], prefix_tail[0],
    )
    attended = attended.reshape(KVH, group, steps, HEAD_SIZE).transpose(2, 0, 1, 3)
    return attended.reshape(queries.shape)


def solution(mesh):
    in_specs = (
        P("prompt", "sample", None, None),
        P("prompt", "sample", None, None, None),
        P("prompt", "sample", None, None, None),
        P("prompt", "sample"),
        P("prompt", "sample", None, None),
        P("prompt", "sample", None, None),
        P(),
    )
    out_specs = P("prompt", "sample", None, None)
    return jax.shard_map(
        per_device, mesh=mesh, in_specs=in_specs, out_specs=out_specs, check_vma=False
    )
```

```python
import functools
import math

import jax
import jax.numpy as jnp
from jax import lax
from jax.experimental import pallas as pl
from jax.experimental.pallas import tpu as pltpu
from jax.sharding import PartitionSpec as P

KVH = 8
HEAD_SIZE = 128
NEG = -1e30
SCALE = math.log2(math.e) * HEAD_SIZE ** (-0.5)
FLOOR = -1e29
PAIR = 1
FEW = 4
MESH = pl.DeviceIdType.MESH
F32 = jnp.float32
BF16 = jnp.bfloat16


def softmax_sums(queries, pairs, bias):
    contract = (((1,), (1,)), ((), ()))
    scores = [
        lax.dot_general(q, p, contract, preferred_element_type=F32) for q, p in zip(queries, pairs)
    ]
    masked = [s * SCALE + bias for s in scores]
    maxima = [jnp.maximum(jnp.max(m, axis=1, keepdims=True), FLOOR) for m in masked]
    weights = [jnp.exp2(m - top) for m, top in zip(masked, maxima)]
    totals = [jnp.sum(w, axis=1, keepdims=True) for w in weights]
    weights = [pltpu.roll(w, 1, 1) for w in weights]
    high = [w.astype(BF16) for w in weights]
    low = [(w - h.astype(F32)).astype(BF16) for w, h in zip(weights, high)]
    numerators = [
        jnp.dot(h, p, preferred_element_type=F32) + jnp.dot(l, p, preferred_element_type=F32)
        for h, l, p in zip(high, low, pairs)
    ]
    return numerators, maxima, totals


def put_stats(stats, lane, head, maxima, totals):
    return jnp.where(lane == head, maxima, jnp.where(lane == KVH + head, totals, stats))


def kernel(
    samples, prompts,
    plen_hbm, slen_hbm, q_hbm, new_ref, suf_ref, head_ref, tail_ref, o_ref,
    plen_ref, slen_ref, q_ref, qall, keys, stage, sufs, nsend, nrecv, ssend, srecv, near,
    asem, lsem, qs_sem, qr_sem, ts_sem, tr_sem, ns_sem, nr_sem, ss_sem, sr_sem,
):
    row, me = lax.axis_index("prompt"), lax.axis_index("sample")
    steps = q_ref.shape[0]
    group = q_ref.shape[1] // (KVH * HEAD_SIZE)
    rows = steps * group
    block = head_ref.shape[0]
    slots = suf_ref.shape[0]
    chunks = KVH // PAIR
    above = lax.rem(row + prompts - 1, prompts)
    below = lax.rem(row + 1, prompts)

    def lanes(g):
        return pl.ds(g * HEAD_SIZE, HEAD_SIZE)

    def local(kind, g):
        source = (tail_ref, suf_ref, new_ref, head_ref)[kind]
        target = (
            lambda: stage.at[g],
            lambda: sufs.at[g, pl.ds(0, slots)],
            lambda: sufs.at[g, pl.ds(slots, steps)],
            lambda: keys.at[g, pl.ds(0, block)],
        )[kind]
        return pltpu.make_async_copy(source.at[:, :, lanes(g)], target(), lsem.at[kind, g])

    arrivals = [
        pltpu.make_async_copy(q_hbm, q_ref, asem.at[0]),
        pltpu.make_async_copy(plen_hbm, plen_ref, asem.at[1]),
        pltpu.make_async_copy(slen_hbm, slen_ref, asem.at[2]),
    ]
    for copy in arrivals:
        copy.start()
    for g in range(KVH):
        local(0, g).start()

    barrier = pltpu.get_barrier_semaphore()
    for d in range(1, samples):
        pl.semaphore_signal(
            barrier, inc=1, device_id=(row, lax.rem(me + d, samples)), device_id_type=MESH
        )
    pl.semaphore_signal(barrier, inc=1, device_id=(above, me), device_id_type=MESH)
    pl.semaphore_signal(barrier, inc=1, device_id=(below, me), device_id_type=MESH)

    spare = sufs.shape[1] - slots
    for g in range(KVH):
        sufs[g, pl.ds(slots, spare)] = jnp.zeros((spare, 2, HEAD_SIZE), BF16)
    for g in range(KVH):
        for kind in range(1, 4):
            local(kind, g).start()

    for copy in arrivals:
        copy.wait()
    wide = q_ref[...].astype(F32)
    for g in range(KVH):
        parts = [
            wide[:, (g * group + x) * HEAD_SIZE : (g * group + x + 1) * HEAD_SIZE]
            for x in range(group)
        ]
        qall[0, g] = jnp.concatenate(parts, axis=0).astype(BF16)

    pl.semaphore_wait(barrier, samples + 1)

    def heads(c):
        return pl.ds(c * PAIR, PAIR)

    def q_copy(d, c):
        return pltpu.make_async_remote_copy(
            src_ref=qall.at[0, heads(c)], dst_ref=qall.at[d, heads(c)],
            send_sem=qs_sem.at[d, c], recv_sem=qr_sem.at[d, c],
            device_id=(row, lax.rem(me + d, samples)), device_id_type=MESH,
        )

    def t_copy(c):
        return pltpu.make_async_remote_copy(
            src_ref=stage.at[heads(c)], dst_ref=keys.at[heads(c), pl.ds(block, block)],
            send_sem=ts_sem.at[c], recv_sem=tr_sem.at[c],
            device_id=(above, me), device_id_type=MESH,
        )

    def n_copy(d, c):
        return pltpu.make_async_remote_copy(
            src_ref=nsend.at[d, heads(c)], dst_ref=nrecv.at[d, heads(c)],
            send_sem=ns_sem.at[d, c], recv_sem=nr_sem.at[d, c],
            device_id=(row, lax.rem(me + samples - d, samples)), device_id_type=MESH,
        )

    def s_copy(d):
        return pltpu.make_async_remote_copy(
            src_ref=ssend, dst_ref=srecv.at[d],
            send_sem=ss_sem.at[d], recv_sem=sr_sem.at[d],
            device_id=(row, lax.rem(me + samples - d, samples)), device_id_type=MESH,
        )

    for c in range(chunks):
        for d in range(1, samples):
            q_copy(d, c).start()
    for c in range(chunks):
        for g in range(c * PAIR, (c + 1) * PAIR):
            local(0, g).wait()
        t_copy(c).start()

    shape = (rows, 2 * sufs.shape[1])
    column = lax.broadcasted_iota(jnp.int32, shape, 1)
    step = lax.rem(lax.broadcasted_iota(jnp.int32, shape, 0), steps)
    place = column // 2
    live = (place < slen_ref[0, 0]) | ((place >= slots) & (place - slots <= step))
    near_bias = jnp.where(live & (lax.rem(column, 2) == 0), 0.0, NEG).astype(F32)
    lane = lax.broadcasted_iota(jnp.int32, (rows, HEAD_SIZE), 1)

    def near_heads(k, stats):
        group_heads = [k * FEW + i for i in range(FEW)]
        for g in group_heads:
            for kind in range(1, 3):
                local(kind, g).wait()
        pairs = [sufs.at[g].reshape(2 * sufs.shape[1], HEAD_SIZE)[...] for g in group_heads]
        sums = softmax_sums([qall[0, g] for g in group_heads], pairs, near_bias)
        for g, numerator, maxima, totals in zip(group_heads, *sums):
            near[g] = numerator
            stats = put_stats(stats, lane, g, maxima, totals)
        return stats

    near_stats = near_heads(0, jnp.zeros((rows, HEAD_SIZE), F32))

    column = lax.broadcasted_iota(jnp.int32, (1, 4 * block), 1)
    place = column // 2
    place = jnp.where(place < block, place + me * block, place + (samples + me - 1) * block)
    far_bias = jnp.where((place < plen_ref[row]) & (lax.rem(column, 2) == 0), 0.0, NEG).astype(F32)
    every = samples * rows
    far_lane = lax.broadcasted_iota(jnp.int32, (every, HEAD_SIZE), 1)

    def far_chunk(c, stats):
        for d in range(1, samples):
            q_copy(d, c).wait_recv()
        t_copy(c).wait_recv()
        both = [c * PAIR + i for i in range(PAIR)]
        for g in both:
            local(3, g).wait()
        pairs = [keys.at[g].reshape(4 * block, HEAD_SIZE)[...] for g in both]
        queries = [qall[:, g].reshape(every, HEAD_SIZE) for g in both]
        sums = softmax_sums(queries, pairs, far_bias)
        for g, numerator, maxima, totals in zip(both, *sums):
            nsend[:, g] = numerator.reshape(samples, rows, HEAD_SIZE)
            stats = put_stats(stats, far_lane, g, maxima, totals)
        for d in range(1, samples):
            n_copy(d, c).start()
        return stats

    far_stats = lax.fori_loop(0, chunks, far_chunk, jnp.full((every, HEAD_SIZE), 0.0, F32))
    ssend[...] = far_stats.T[: 2 * KVH]
    for d in range(1, samples):
        s_copy(d).start()
    for k in range(1, KVH // FEW):
        near_stats = near_heads(k, near_stats)
    padding = jnp.zeros((HEAD_SIZE - rows, HEAD_SIZE), F32)
    near_stats = jnp.concatenate([near_stats, padding], axis=0).T[: 2 * KVH]
    for d in range(1, samples):
        s_copy(d).wait_recv()

    stats = [near_stats, ssend[:, :HEAD_SIZE]]
    for d in range(1, samples):
        stats.append(pltpu.roll(srecv[d], every - d * rows, 1)[:, :HEAD_SIZE])
    peak = functools.reduce(jnp.maximum, [s[:KVH] for s in stats])
    factors = [jnp.exp2(s[:KVH] - peak) for s in stats]
    total = sum(s[KVH:] * f for s, f in zip(stats, factors))
    factors = [f / total for f in factors]
    factors = jnp.concatenate(factors, axis=0).T[:rows]

    def factor(k, g):
        return factors[:, k * KVH + g : k * KVH + g + 1]

    for c in range(chunks):
        for d in range(1, samples):
            n_copy(d, c).wait_recv()
        for g in range(c * PAIR, (c + 1) * PAIR):
            result = near[g] * factor(0, g) + nsend[0, g] * factor(1, g)
            for d in range(1, samples):
                result = result + nrecv[d, g] * factor(d + 1, g)
            o_ref[g] = result.astype(BF16)

    for c in range(chunks):
        t_copy(c).wait_send()
        for d in range(1, samples):
            q_copy(d, c).wait_send()
            n_copy(d, c).wait_send()
    for d in range(1, samples):
        s_copy(d).wait_send()


def per_device(queries, new_kv, suffix_kv, suffix_len, prefix_head, prefix_tail, prefix_len):
    samples = lax.axis_size("sample")
    prompts = lax.axis_size("prompt")
    steps, width = queries.shape[2:]
    group = width // (KVH * HEAD_SIZE)
    rows = steps * group
    block = prefix_head.shape[1]
    slots = suffix_kv.shape[2]
    chunks = KVH // PAIR
    near_len = slots + HEAD_SIZE // 2
    sem = pltpu.SemaphoreType.DMA
    attended = pl.pallas_call(
        functools.partial(kernel, samples, prompts),
        out_shape=jax.ShapeDtypeStruct((KVH, rows, HEAD_SIZE), BF16),
        in_specs=[pl.BlockSpec(memory_space=pl.ANY)] * 7,
        out_specs=pl.BlockSpec(memory_space=pltpu.VMEM),
        scratch_shapes=[
            pltpu.SMEM(prefix_len.shape, jnp.int32),
            pltpu.SMEM(suffix_len.shape, jnp.int32),
            pltpu.VMEM((steps, width), BF16),
            pltpu.VMEM((samples, KVH, rows, HEAD_SIZE), BF16),
            pltpu.VMEM((KVH, 2 * block, 2, HEAD_SIZE), BF16),
            pltpu.VMEM((KVH, block, 2, HEAD_SIZE), BF16),
            pltpu.VMEM((KVH, near_len, 2, HEAD_SIZE), BF16),
            pltpu.VMEM((samples, KVH, rows, HEAD_SIZE), F32),
            pltpu.VMEM((samples, KVH, rows, HEAD_SIZE), F32),
            pltpu.VMEM((2 * KVH, samples * rows), F32),
            pltpu.VMEM((samples, 2 * KVH, samples * rows), F32),
            pltpu.VMEM((KVH, rows, HEAD_SIZE), F32),
            sem((3,)), sem((4, KVH)),
            sem((samples, chunks)), sem((samples, chunks)),
            sem((chunks,)), sem((chunks,)),
            sem((samples, chunks)), sem((samples, chunks)),
            sem((samples,)), sem((samples,)),
        ],
        compiler_params=pltpu.CompilerParams(
            collective_id=0, has_side_effects=True, vmem_limit_bytes=64 * 1024 * 1024
        ),
    )(
        prefix_len, suffix_len, queries[0, 0], new_kv[0, 0], suffix_kv[0, 0],
        prefix_head[0], prefix_tail[0],
    )
    attended = attended.reshape(KVH, group, steps, HEAD_SIZE).transpose(2, 0, 1, 3)
    return attended.reshape(queries.shape)


def solution(mesh):
    in_specs = (
        P("prompt", "sample", None, None),
        P("prompt", "sample", None, None, None),
        P("prompt", "sample", None, None, None),
        P("prompt", "sample"),
        P("prompt", "sample", None, None),
        P("prompt", "sample", None, None),
        P(),
    )
    out_specs = P("prompt", "sample", None, None)
    return jax.shard_map(
        per_device, mesh=mesh, in_specs=in_specs, out_specs=out_specs, check_vma=False
    )
```
